32 devices in a mesh: tx: 4 (over y, core), ty: 8 (over z, x).
Axes of the slice: x: 2, y: 2, z: 4, core: 2. Of those that a mesh axis runs over, the one named last changes fastest.
Arguments:
- increments: bfloat16 [3, 8, 576, 2048], P(None, None, 'tx', 'ty'), may hold values from -6 to 6
- remap_weights: bfloat16 [4, 8, 144, 2, 128, 256], P('tx', 'ty'), may hold values from -0.375 to 0.375
- dest_offset: int32 [4, 8, 144, 2], P('tx', 'ty'), may hold values from 0 to 3, as said below
- slot_patch: int32 [4, 8, 4, 108], P('tx', 'ty'), may hold values from 0 to 143, as said below
- rotation: int32 [2, 4], replicated, may hold values from 0 to 3
- basis: float32 [4, 384, 1536], P(None, 'ty', 'tx'), may hold values from -4 to 4
- inv_metric_diag: float32 [2, 384, 1536], P(None, 'ty', 'tx'), may hold values from 0.7 to 1.7
- inv_metric_cross: float32 [384, 1536], P('ty', 'tx'), may hold values from -0.5 to 0.5
- thickness: float32 [8, 384, 1536], P(None, 'ty', 'tx'), may hold values from -6 to 6
- wind_first: float32 [8, 384, 1536], P(None, 'ty', 'tx'), may hold values from -6 to 6
- wind_second: float32 [8, 384, 1536], P(None, 'ty', 'tx'), may hold values from -6 to 6
Outputs:
- thickness_new: float32 [8, 384, 1536], P(None, 'ty', 'tx')
- wind_first_new: float32 [8, 384, 1536], P(None, 'ty', 'tx')
- wind_second_new: float32 [8, 384, 1536], P(None, 'ty', 'tx')
The draws below stay inside these ranges and needn't reach their ends.
Inputs may be any that keep to these rules, and one draw needn't show every extreme that they name: `dest_offset`: the intersections of one block name every one of the 4 distances at least 36 and at most 108 times, and one of them exactly 108 times. In every tx row some tile owner receives exactly 108 intersections from each of the 4 blocks that send to it. `slot_patch`: slots past the number of intersections that arrive from a sender receive nothing. The used slots of one tile owner name every one of its 144 patches at least once.
All inputs are finite; a program needn't handle non-finite values.
Results may differ from the reference program's by a relative error of at most 0.0003.
Values sent between devices are 32-bit elements; how exact they have to be, the bound alone decides.
No kernel may reach another device: no remote copies, remote signals or barrier semaphores. Data moves between devices by JAX's collectives and lax.ppermute only.
A program may use at most 192 MiB of HBM per device.

```python
import jax
import jax.numpy as jnp
from jax import lax

L = 8
PANELS = 4
STEPS = 4
TC = 384
TR = 48
TPATCH = 128
SC = 256
TOP = 2
OWNERS = 4
TP = 144
SR = 144
LO = 36
CAP = 108
NR = 384
NC = 1536
LATS = 576
LONS = 2048
N_TX = 4
N_TY = 8


def intersection_plan(key):
    base_key = jax.random.fold_in(key, 11)
    subkeys = jax.random.split(base_key, 6)
    offsets = jnp.arange(OWNERS, dtype=jnp.int32)
    heavy_offset = jax.random.randint(subkeys[0], (N_TX, N_TY), 0, OWNERS)
    chosen = jax.random.randint(subkeys[1], (N_TX, 1), 0, N_TY)
    columns = jnp.arange(N_TY, dtype=jnp.int32)[None, :]
    forced = (chosen - columns) % N_TY
    heavy_offset = jnp.where(forced < OWNERS, forced, heavy_offset)
    pick_ids = jax.random.randint(subkeys[2], (N_TX, N_TY, 2 * LO), 0, OWNERS - 1)
    pick_ids = pick_ids + (pick_ids >= heavy_offset[:, :, None]).astype(jnp.int32)
    extra_count = jnp.sum((pick_ids[:, :, :, None] == offsets[None, None, None, :]).astype(jnp.int32), axis=2)
    counts = jnp.where(offsets[None, None, :] == heavy_offset[:, :, None], CAP, LO + extra_count).astype(jnp.int32)
    return (counts, subkeys)


def draw_dest_offset(key, part):
    counts, subkeys = intersection_plan(key)
    entries = SR * TOP
    bounds = jnp.cumsum(counts, axis=2).astype(jnp.int32)
    entry_ids = jnp.arange(entries, dtype=jnp.int32)
    ordered = jnp.sum((entry_ids[None, None, :, None] >= bounds[:, :, None, :OWNERS - 1]).astype(jnp.int32), axis=3)
    shuffles = jax.vmap(lambda one_key: jax.random.permutation(one_key, entries))(jax.random.split(subkeys[3], N_TX * N_TY))
    shuffles = shuffles.reshape(N_TX, N_TY, entries).astype(jnp.int32)
    return jnp.take_along_axis(ordered, shuffles, axis=2).reshape(N_TX, N_TY, SR, TOP).astype(jnp.int32)


def draw_slot_patch(key, part):
    counts, subkeys = intersection_plan(key)
    offsets = jnp.arange(OWNERS, dtype=jnp.int32)
    sources = (jnp.arange(N_TY, dtype=jnp.int32)[:, None] - offsets[None, :]) % N_TY
    arriving = counts[:, sources, offsets[None, :]]
    starts = (jnp.cumsum(arriving, axis=2) - arriving).astype(jnp.int32)
    slots = jnp.arange(CAP, dtype=jnp.int32)
    running = starts[:, :, :, None] + slots[None, None, None, :]
    shuffles = jax.vmap(lambda one_key: jax.random.permutation(one_key, TP))(jax.random.split(subkeys[4], N_TX * N_TY))
    shuffles = shuffles.reshape(N_TX, N_TY, TP).astype(jnp.int32)
    used = jnp.take_along_axis(shuffles, (running % TP).reshape(N_TX, N_TY, OWNERS * CAP), axis=2).reshape(N_TX, N_TY, OWNERS, CAP)
    filler = jax.random.randint(subkeys[5], (N_TX, N_TY, OWNERS, CAP), 0, TP)
    return jnp.where(slots[None, None, None, :] < arriving[:, :, :, None], used, filler).astype(jnp.int32)


def set_ends(values, stream_key, least, largest):
    index_at = [jax.random.randint(jax.random.fold_in(stream_key, axis), (), 0, length) for axis, length in enumerate(values.shape)]
    main_axis = values.shape.index(max(values.shape))
    next_to = index_at[:main_axis] + [(index_at[main_axis] + 1) % values.shape[main_axis]] + index_at[main_axis + 1:]
    return values.at[tuple(index_at)].set(least).at[tuple(next_to)].set(largest)


def steps_of(key, shape, cuts, smallest, top_value):
    def one(dim, shards_of):
        heights = jax.random.uniform(jax.random.fold_in(jax.random.fold_in(key, 6), dim), (shards_of,), jnp.float32, smallest / len(cuts), top_value / len(cuts))
        return jnp.repeat(jnp.exp(heights), shape[dim] // shards_of).reshape((-1,) + (1,) * (len(shape) - dim - 1))

    gain = one(*cuts[0])
    for cut in cuts[1:]:
        gain = gain * one(*cut)
    return gain


def gaussian(key, shape, width, reach, shards=(), kind=jnp.bfloat16):
    result = jax.random.normal(key, shape, jnp.float32) * width
    if len(shards) > 0:
        result = steps_of(key, shape, shards, -0.22, 0.18) * result
    return jnp.clip(result, min=-reach, max=reach).astype(kind)


def setup_inputs(seed: int = 0) -> dict:
    seeds = jax.random.split(jax.random.key(seed), 12)
    return {
        "increments": gaussian(seeds[0], (3, L, LATS, LONS), 1.0, 6.0, ((2, 4), (3, 8))),
        "remap_weights": gaussian(seeds[1], (N_TX, N_TY, SR, TOP, TPATCH, SC), SC ** -0.5, 0.375, ((0, 4), (1, 8))),
        "dest_offset": draw_dest_offset(jax.random.fold_in(seeds[11], 71), 0),
        "slot_patch": draw_slot_patch(jax.random.fold_in(seeds[11], 71), 0),
        "rotation": set_ends(jax.random.randint(seeds[4], (2, PANELS), 0, 4), jax.random.fold_in(seeds[4], 1), 0, 3).astype(jnp.int32),
        "basis": gaussian(seeds[5], (4, NR, NC), 1.0, 4.0, ((1, 8), (2, 4)), jnp.float32),
        "inv_metric_diag": jnp.clip(0.7 + 1 * jax.random.uniform(seeds[6], (2, NR, NC), jnp.float32) ** steps_of(seeds[6], (2, NR, NC), ((1, 8), (2, 4)), -0.2, 0.2), 0.7, 1.7),
        "inv_metric_cross": jnp.clip(jax.random.uniform(seeds[7], (NR, NC), jnp.float32, -0.5, 0.5) * steps_of(seeds[7], (NR, NC), ((0, 8), (1, 4)), -0.4, 0.0), -0.5, 0.5),
        "thickness": gaussian(seeds[8], (L, NR, NC), 1.0, 6.0, ((1, 8), (2, 4)), jnp.float32),
        "wind_first": gaussian(seeds[9], (L, NR, NC), 1.0, 6.0, ((1, 8), (2, 4)), jnp.float32),
        "wind_second": gaussian(seeds[10], (L, NR, NC), 1.0, 6.0, ((1, 8), (2, 4)), jnp.float32),
    }


COURANT = 0.15
GRADIENT = 0.3


def quarter_turn(code):
    cosine = (code == 0).astype(jnp.float32) - (code == 2).astype(jnp.float32)
    sine_value = (code == 1).astype(jnp.float32) - (code == 3).astype(jnp.float32)
    return cosine, sine_value


def advance(depth, cov_first, cov_second, con_first, con_second, depth_below, second_below, depth_above, second_above, depth_left, first_left, depth_right, first_right, wall_left, wall_right):
    face_below = 0.5 * (con_second + second_below)
    flux_below = jnp.maximum(face_below, 0.0) * depth_below + jnp.minimum(face_below, 0.0) * depth
    face_above = 0.5 * (con_second + second_above)
    flux_above = jnp.maximum(face_above, 0.0) * depth + jnp.minimum(face_above, 0.0) * depth_above
    face_left = 0.5 * (con_first + first_left) * wall_left
    flux_left = jnp.maximum(face_left, 0.0) * depth_left + jnp.minimum(face_left, 0.0) * depth
    face_right = 0.5 * (con_first + first_right) * wall_right
    flux_right = jnp.maximum(face_right, 0.0) * depth + jnp.minimum(face_right, 0.0) * depth_right
    new_depth = depth - COURANT * ((flux_right - flux_left) + (flux_above - flux_below))
    new_first = cov_first - GRADIENT * 0.5 * (depth_right - depth_left)
    new_second = cov_second - GRADIENT * 0.5 * (depth_above - depth_below)
    return new_depth, new_first, new_second


def reference(increments, remap_weights, dest_offset, slot_patch, rotation, basis, inv_metric_diag, inv_metric_cross, thickness, wind_first, wind_second):
    row_width = 3 * L * TPATCH
    entries = SR * TOP
    block_count = N_TX * N_TY
    blocks = increments.reshape(3, L, N_TX, SR, N_TY, SC).transpose(2, 4, 0, 1, 3, 5).reshape(block_count, 3, L, SR, SC)
    weights = remap_weights.reshape(block_count, SR, TOP, TPATCH, SC)

    def one_block(pair):
        block, weight = pair
        partial_terms = jnp.einsum("clsk,stpk->stclp", block.astype(jnp.float32), weight.astype(jnp.float32))
        return partial_terms.reshape(entries, row_width)

    contrib = lax.map(one_block, (blocks, weights))
    block_ids = jnp.arange(block_count, dtype=jnp.int32)
    tile_row = block_ids // N_TY
    tile_col = block_ids % N_TY
    offsets = dest_offset.reshape(block_count, entries).astype(jnp.int32)
    onehot = (offsets[:, :, None] == jnp.arange(OWNERS, dtype=jnp.int32)[None, None, :]).astype(jnp.int32)
    earlier = (jnp.cumsum(onehot, axis=1) - onehot).astype(jnp.int32)
    slot_index = jnp.sum(earlier * onehot, axis=2).astype(jnp.int32)
    receiver = ((tile_col[:, None] + offsets) % N_TY).astype(jnp.int32)
    patch_id = slot_patch[tile_row[:, None], receiver, offsets, slot_index].astype(jnp.int32)
    target = ((tile_row[:, None] * N_TY + receiver) * TP + patch_id).reshape(-1).astype(jnp.int32)
    patches = jnp.zeros((block_count * TP, row_width), jnp.float32).at[target].add(contrib.reshape(-1, row_width))
    blocks_per_row = TC // TPATCH
    tiles = patches.reshape(N_TX, N_TY, TR, blocks_per_row, 3, L, TPATCH).transpose(4, 5, 1, 2, 0, 3, 6).reshape(3, L, NR, NC)
    cov_first = wind_first + basis[0] * tiles[0] + basis[1] * tiles[1]
    cov_second = wind_second + basis[2] * tiles[0] + basis[3] * tiles[1]
    depth = thickness + tiles[2]

    rows_all = jnp.arange(NR, dtype=jnp.int32)
    panel_rows = NR // PANELS
    panel = rows_all // panel_rows
    code_below = jnp.where(rows_all % panel_rows == 0, rotation[0][panel], 0)
    code_above = jnp.where(rows_all % panel_rows == panel_rows - 1, rotation[1][panel], 0)
    cos_below, sin_below = quarter_turn(code_below[:, None])
    cos_above, sin_above = quarter_turn(code_above[:, None])
    columns = jnp.arange(NC, dtype=jnp.int32)
    wall_left = jnp.where(columns == 0, 0.0, 1.0).astype(jnp.float32)
    wall_right = jnp.where(columns == NC - 1, 0.0, 1.0).astype(jnp.float32)
    zero_column = jnp.zeros((L, NR, 1), jnp.float32)

    for iteration in range(STEPS):
        con_first = inv_metric_diag[0] * cov_first + inv_metric_cross * cov_second
        con_second = inv_metric_cross * cov_first + inv_metric_diag[1] * cov_second
        depth_below = jnp.roll(depth, 1, axis=1)
        second_below = sin_below * jnp.roll(con_first, 1, axis=1) + cos_below * jnp.roll(con_second, 1, axis=1)
        depth_above = jnp.roll(depth, -1, axis=1)
        second_above = sin_above * jnp.roll(con_first, -1, axis=1) + cos_above * jnp.roll(con_second, -1, axis=1)
        depth_left = jnp.concatenate([zero_column, depth[:, :, :-1]], axis=2)
        first_left = jnp.concatenate([zero_column, con_first[:, :, :-1]], axis=2)
        depth_right = jnp.concatenate([depth[:, :, 1:], zero_column], axis=2)
        first_right = jnp.concatenate([con_first[:, :, 1:], zero_column], axis=2)
        depth, cov_first, cov_second = advance(depth, cov_first, cov_second, con_first, con_second, depth_below, second_below, depth_above, second_above, depth_left, first_left, depth_right, first_right, wall_left, wall_right)
    return depth, cov_first, cov_second
```

```python
import functools

import jax
import jax.numpy as jnp
from jax import lax
from jax.experimental import pallas as pl
from jax.experimental.pallas import tpu as pltpu
from jax.sharding import PartitionSpec as P

PANELS = 4
STEPS = 4
TPATCH = 128
HALO = 4
SUB = 8
FIELDS = 3
COURANT = 0.15
GRADIENT = 0.3
CHUNKS = (4, 4)
GROUP = 16
VMEM = 61 * 2**20

ROWS_BY_ROWS = (((1,), (1,)), ((), ()))


def params(limit=VMEM):
    return pltpu.CompilerParams(vmem_limit_bytes=limit)


def in_vmem(count):
    return [pl.BlockSpec(memory_space=pltpu.VMEM)] * count


def in_smem(count):
    return [pl.BlockSpec(memory_space=pltpu.SMEM)] * count


def in_hbm(count):
    return [pl.BlockSpec(memory_space=pl.ANY)] * count


def terms_kernel(bounds, group, offsets, increments, weights, *refs):
    parts = len(bounds) - 1
    fields, levels, rows, width = increments.shape
    count = fields * levels
    pieces, tops = weights.shape[1] // TPATCH, offsets.shape[3]
    outs = refs[: -9]
    owners = len(outs) // parts
    capacity = outs[0].shape[0] // (fields * (bounds[1] - bounds[0]))
    held, source, left, right, slots, used, source_sem, held_sem, out_sem = refs[-9:]
    groups = rows // group

    first = pltpu.make_async_copy(increments, source, source_sem)
    first.start()

    def fetch(g):
        piece = pl.ds(g * group, group)
        return pltpu.make_async_copy(weights.at[piece], held.at[piece], held_sem.at[g])

    @pl.loop(0, groups)
    def _(g):
        fetch(g).start()

    for o in range(owners):
        used[o] = 0
    slots[...] = jnp.zeros_like(slots)
    first.wait()
    half = width // 2
    for l in range(levels):
        for c in range(fields):
            at = pl.ds((l * fields + c) * rows, rows)
            left[at, :] = source[c, l, :, :half].astype(jnp.float32)
            right[at, :] = source[c, l, :, half:].astype(jnp.float32)

    @pl.loop(0, groups)
    def _(g):
        fetch(g).wait()
        for j in range(group):
            s = g * group + j
            at = pl.ds(s, count, stride=rows)
            block = jnp.concatenate([left[at, :], right[at, :]], axis=1).astype(jnp.bfloat16)
            term = lax.dot_general(block, held[s], ROWS_BY_ROWS, preferred_element_type=jnp.float32)
            for t in range(tops):
                o = offsets[0, 0, s, t]
                k = used[o]
                used[o] = k + 1
                slots[pl.ds(o * (count * capacity) + k, count, stride=capacity), :] = term[
                    :, t * TPATCH : (t + 1) * TPATCH
                ]

    copies = []
    for o in range(owners):
        for j in range(parts):
            size = fields * (bounds[j + 1] - bounds[j]) * capacity
            start = (o * count + fields * bounds[j]) * capacity
            copy = pltpu.make_async_copy(
                slots.at[pl.ds(start, size)], outs[o * parts + j], out_sem.at[o * parts + j]
            )
            copy.start()
            copies.append(copy)
    for copy in copies:
        copy.wait()


def terms(bounds, owners, capacity, offsets, increments, weights):
    parts = len(bounds) - 1
    fields, levels, rows, width = increments.shape
    count = fields * levels
    group = max(g for g in range(1, GROUP + 1) if rows % g == 0)
    out = pl.pallas_call(
        functools.partial(terms_kernel, bounds, group),
        in_specs=in_smem(1) + in_hbm(2),
        out_specs=in_hbm(owners * parts),
        out_shape=[
            jax.ShapeDtypeStruct((fields * (bounds[j + 1] - bounds[j]) * capacity, TPATCH), jnp.float32)
            for _ in range(owners)
            for j in range(parts)
        ],
        scratch_shapes=[
            pltpu.VMEM(weights.shape, jnp.bfloat16),
            pltpu.VMEM(increments.shape, jnp.bfloat16),
            pltpu.VMEM((count * rows, width // 2), jnp.float32),
            pltpu.VMEM((count * rows, width // 2), jnp.float32),
            pltpu.VMEM((owners * count * capacity, TPATCH), jnp.float32),
            pltpu.SMEM((owners,), jnp.int32),
            pltpu.SemaphoreType.DMA,
            pltpu.SemaphoreType.DMA((rows // group,)),
            pltpu.SemaphoreType.DMA((owners * parts,)),
        ],
        compiler_params=params(),
        name="terms",
    )(offsets, increments, weights)
    return [out[o * parts : (o + 1) * parts] for o in range(owners)]


def add_slots(total, slots, places, which, count, patches):
    capacity = slots.shape[0] // count

    def one(k, carry):
        at = pl.ds(places[which, k], count, stride=patches)
        total[at, :] = total[at, :] + slots[pl.ds(k, count, stride=capacity), :]
        return carry

    lax.fori_loop(0, capacity, one, 0, unroll=4)


def gather_kernel(which, whole, count, patches, places, *refs):
    total = refs[-1]
    if whole:
        total[...] = refs[0][...]
        for i in range(1, whole):
            total[...] += refs[i][...]
    else:
        total[...] = jnp.zeros_like(total)
    for row, slots in zip(which, refs[whole:-1]):
        add_slots(total, slots, places, row, count, patches)


def gathered(places, wholes, slot_arrays, which, count, patches):
    return pl.pallas_call(
        functools.partial(gather_kernel, which, len(wholes), count, patches),
        in_specs=in_smem(1) + in_vmem(len(wholes) + len(slot_arrays)),
        out_specs=in_vmem(1)[0],
        out_shape=jax.ShapeDtypeStruct((count * patches, TPATCH), jnp.float32),
        compiler_params=params(24 * 2**20),
        name="gather_patches",
    )(places, *wholes, *slot_arrays)


def fields_kernel(levels, patches, odd, places, last, across, direct, own, basis, thickness, wind_first, wind_second, *refs):
    depth, cov_first, cov_second, low_rows, high_rows, low_cols, high_cols, total = refs
    rows, cols = depth.shape[1:]
    blocks = cols // TPATCH
    count = FIELDS * levels
    total[...] = last[...]

    @pl.when(odd[0] == 1)
    def _():
        total[...] += across[...]
        add_slots(total, direct, places, 2, count, patches)

    add_slots(total, own, places, 0, count, patches)
    lane = lax.broadcasted_iota(jnp.int32, (rows, TPATCH), 1)
    low, high = jnp.zeros((rows, TPATCH), jnp.float32), jnp.zeros((rows, TPATCH), jnp.float32)
    for l in range(levels):
        for block in range(blocks):
            at = slice(block * TPATCH, (block + 1) * TPATCH)
            east, north, thick = (
                total[(l * FIELDS + c) * patches + block * rows : (l * FIELDS + c) * patches + (block + 1) * rows, :]
                for c in range(FIELDS)
            )
            values = (
                thickness[l, :, at] + thick,
                wind_first[l, :, at] + basis[0, :, at] * east + basis[1, :, at] * north,
                wind_second[l, :, at] + basis[2, :, at] * east + basis[3, :, at] * north,
            )
            for f, (ref, value) in enumerate(zip((depth, cov_first, cov_second), values)):
                ref[l, :, at] = value
                i = f * levels + l
                low_rows[i * HALO : (i + 1) * HALO, at] = value[:HALO]
                high_rows[i * HALO : (i + 1) * HALO, at] = value[rows - HALO :]
                here = (lane >= i * HALO) & (lane < (i + 1) * HALO)
                if block == 0:
                    low = jnp.where(here, pltpu.roll(value, i * HALO, 1), low)
                if block == blocks - 1:
                    high = jnp.where(here, pltpu.roll(value, (i + 1) * HALO, 1), high)
    low_cols[...] = low
    high_cols[...] = high


def first_fields(levels, patches, odd, places, last, across, direct, own, basis, thickness, wind_first, wind_second):
    rows, cols = thickness.shape[1:]
    count = FIELDS * levels
    whole = jax.ShapeDtypeStruct((levels, rows, cols), jnp.float32)
    ends = jax.ShapeDtypeStruct((count * HALO, cols), jnp.float32)
    sides = jax.ShapeDtypeStruct((rows, TPATCH), jnp.float32)
    return pl.pallas_call(
        functools.partial(fields_kernel, levels, patches),
        in_specs=in_smem(2) + in_vmem(8),
        out_specs=in_vmem(7),
        out_shape=[whole, whole, whole, ends, ends, sides, sides],
        scratch_shapes=[pltpu.VMEM((count * patches, TPATCH), jnp.float32)],
        compiler_params=params(32 * 2**20),
        name="first_fields",
    )(odd, places, last, across, direct, own, basis, thickness, wind_first, wind_second)


def steps_kernel(levels, metric, turns, wall, from_below, from_above, from_left, from_right, *refs):
    parts, outs = refs[:FIELDS], refs[-FIELDS:]
    rows, cols = parts[0].shape[1:]
    count = FIELDS * levels
    ext_rows, ext_cols = rows + SUB, cols + TPATCH

    def side(own, at):
        lanes = slice(at * TPATCH, (at + 1) * TPATCH)
        ends = [ref[count * HALO : (count + 1) * HALO, lanes] for ref in (from_above, from_below)]
        return jnp.concatenate([own[...]] + ends, axis=0)

    left, right = side(from_left, 0), side(from_right, 1)
    lane = lax.broadcasted_iota(jnp.int32, (ext_rows, TPATCH), 1)

    for l in range(levels):
        values = []
        for f in range(FIELDS):
            i = f * levels + l
            at = slice(i * HALO, (i + 1) * HALO)
            ends = jnp.concatenate([from_above[at, :], from_below[at, :]], axis=0)
            rim = jnp.where(
                lane < HALO,
                pltpu.roll(right, (TPATCH - i * HALO) % TPATCH, 1),
                jnp.where(lane >= TPATCH - HALO, pltpu.roll(left, (TPATCH - (i + 1) * HALO) % TPATCH, 1), 0.0),
            )
            values.append(
                jnp.concatenate([jnp.concatenate([parts[f][l], ends], axis=0), rim], axis=1)
            )
        depth, cov_first, cov_second = values
        cos_below, sin_below, cos_above, sin_above = (
            jnp.concatenate([turns[i]] * (ext_cols // TPATCH), axis=1) for i in range(4)
        )
        for _ in range(STEPS):
            con_first = metric[0] * cov_first + metric[2] * cov_second
            con_second = metric[2] * cov_first + metric[1] * cov_second
            before, after = functools.partial(pltpu.roll, shift=1), lambda v, axis: pltpu.roll(v, v.shape[axis] - 1, axis)
            depth_below, depth_above = before(depth, axis=0), after(depth, 0)
            second_below = sin_below * before(con_first, axis=0) + cos_below * before(con_second, axis=0)
            second_above = sin_above * after(con_first, 0) + cos_above * after(con_second, 0)
            face_below = 0.5 * (con_second + second_below)
            flux_below = jnp.maximum(face_below, 0.0) * depth_below + jnp.minimum(face_below, 0.0) * depth
            face_above = 0.5 * (con_second + second_above)
            flux_above = jnp.maximum(face_above, 0.0) * depth + jnp.minimum(face_above, 0.0) * depth_above
            depth_left, depth_right = before(depth, axis=1), after(depth, 1)
            face_left = 0.5 * (con_first + before(con_first, axis=1)) * wall[0:1, :]
            flux_left = jnp.maximum(face_left, 0.0) * depth_left + jnp.minimum(face_left, 0.0) * depth
            flux_right = after(flux_left, 1)
            depth = depth - COURANT * ((flux_right - flux_left) + (flux_above - flux_below))
            cov_first = cov_first - GRADIENT * 0.5 * (depth_right - depth_left)
            cov_second = cov_second - GRADIENT * 0.5 * (depth_above - depth_below)
        for ref, value in zip(outs, (depth, cov_first, cov_second)):
            ref[l] = value[:rows, :cols]


def steps(levels, metric, turns, wall, halos, parts):
    rows, cols = parts[0].shape[1:]
    return pl.pallas_call(
        functools.partial(steps_kernel, levels),
        in_specs=in_vmem(7 + FIELDS),
        out_specs=in_vmem(FIELDS),
        out_shape=[jax.ShapeDtypeStruct((levels, rows, cols), jnp.float32)] * FIELDS,
        compiler_params=params(32 * 2**20),
        name="steps",
    )(metric, turns, wall, *halos, *parts)


def quarter_turn(code):
    cosine = (code == 0).astype(jnp.float32) - (code == 2).astype(jnp.float32)
    sine_value = (code == 1).astype(jnp.float32) - (code == 3).astype(jnp.float32)
    return (cosine, sine_value)


def turn_factors(first_row, rows, total_rows, rotation):
    index = jnp.arange(rows + SUB, dtype=jnp.int32)
    index = jnp.where(index < rows + HALO, index, index - rows - SUB)
    row = (first_row + index) % total_rows
    panel_rows = total_rows // PANELS
    matches = jnp.arange(PANELS, dtype=jnp.int32)[None, :] == (row // panel_rows)[:, None]
    lower = jnp.sum(jnp.where(matches, rotation[0][None, :], 0), axis=1)
    upper = jnp.sum(jnp.where(matches, rotation[1][None, :], 0), axis=1)
    below = jnp.where(row % panel_rows == 0, lower, 0)
    above = jnp.where(row % panel_rows == panel_rows - 1, upper, 0)
    factors = jnp.stack(quarter_turn(below) + quarter_turn(above))
    return jnp.broadcast_to(factors[:, :, None], factors.shape + (TPATCH,))


def shift(array, axis, by, closed):
    size = lax.axis_size(axis)
    pairs = [(i, (i + by) % size) for i in range(size) if closed or 0 <= i + by < size]
    return lax.ppermute(array, axis, pairs)


def rimmed(array):
    rows, cols = array.shape[1:]
    below = shift(array[:, rows - HALO :], "ty", 1, True)
    above = shift(array[:, :HALO], "ty", -1, True)
    array = jnp.concatenate([array, above, below], axis=1)
    left = shift(array[:, :, cols - HALO :], "tx", 1, False)
    right = shift(array[:, :, :HALO], "tx", -1, False)
    gap = jnp.zeros(array.shape[:2] + (TPATCH - 2 * HALO,), array.dtype)
    return jnp.concatenate([array, right, gap, left], axis=2)


def body(
    increments,
    remap_weights,
    dest_offset,
    slot_patch,
    rotation,
    basis,
    inv_metric_diag,
    inv_metric_cross,
    thickness,
    wind_first,
    wind_second,
):
    levels, rows, cols = thickness.shape
    tx_count, ty_count = lax.axis_size("tx"), lax.axis_size("ty")
    tx_index, ty_index = lax.axis_index("tx"), lax.axis_index("ty")
    owners, capacity = slot_patch.shape[2:]
    blocks = cols // TPATCH
    patches = rows * blocks
    bounds = [0]
    while bounds[-1] < levels:
        bounds.append(min(levels, bounds[-1] + CHUNKS[len(bounds) - 1]))
    parts = len(bounds) - 1

    evens, odds = range(0, ty_count, 2), range(1, ty_count, 2)
    swap = [(b, b + 1) for b in evens] + [(b, b - 1) for b in odds]
    on_even = [(b, (b + 2) % ty_count) for b in evens]
    on_odd = [(b, (b + 2) % ty_count) for b in odds]
    send = lambda array, pairs: lax.ppermute(array, "ty", pairs)

    places = slot_patch[0, 0]
    places = (places % blocks) * rows + places // blocks
    places_next = shift(places, "ty", -1, True)
    places_second = shift(places, "ty", -2, True)
    odd = (ty_index % 2).reshape(1)

    metric = rimmed(jnp.concatenate([inv_metric_diag, inv_metric_cross[None]], axis=0))
    turns = turn_factors(ty_index * rows, rows, rows * ty_count, rotation)
    column = jnp.arange(cols + TPATCH, dtype=jnp.int32)
    column = tx_index * cols + jnp.where(column < cols + TPATCH // 2, column, column - cols - TPATCH)
    wall = jnp.where((column == 0) | (column == cols * tx_count), 0.0, 1.0).astype(jnp.float32)
    wall = jnp.broadcast_to(wall[None, :], (SUB, cols + TPATCH))

    slots = terms(
        bounds, owners, capacity, dest_offset, increments,
        remap_weights.reshape(increments.shape[2], -1, remap_weights.shape[-1]),
    )
    results = []
    for j in range(parts):
        size = bounds[j + 1] - bounds[j]
        count = FIELDS * size
        third = send(slots[3][j], on_even + on_odd)
        direct = send(slots[2][j], on_odd)
        paired = gathered(places_next, [], [third, slots[1][j]], (3, 1), count, patches)
        across = send(paired, swap)
        joined = gathered(places_second, [across], [slots[2][j]], (2,), count, patches)
        last = send(joined, on_even)
        *fields, low_rows, high_rows, low_cols, high_cols = first_fields(
            size, patches, odd, places, last, across, direct, slots[0][j], basis,
            *(a[bounds[j] : bounds[j + 1]] for a in (thickness, wind_first, wind_second)),
        )
        from_left = shift(high_cols, "tx", 1, False)
        from_right = shift(low_cols, "tx", -1, False)

        def with_corners(ends, at):
            corners = [a[at : at + HALO] for a in (from_left, from_right)]
            corners.append(jnp.zeros((HALO, cols - 2 * TPATCH), jnp.float32))
            return jnp.concatenate([ends, jnp.concatenate(corners, axis=1)], axis=0)

        from_below = shift(with_corners(high_rows, rows - HALO), "ty", 1, True)
        from_above = shift(with_corners(low_rows, 0), "ty", -1, True)
        results.append(
            steps(size, metric, turns, wall, (from_below, from_above, from_left, from_right), fields)
        )
    return tuple(jnp.concatenate(field, axis=0) for field in zip(*results))


def solution(mesh):
    in_specs = (
        P(None, None, "tx", "ty"),
        P("tx", "ty", None, None, None, None),
        P("tx", "ty", None, None),
        P("tx", "ty", None, None),
        P(),
        P(None, "ty", "tx"),
        P(None, "ty", "tx"),
        P("ty", "tx"),
        P(None, "ty", "tx"),
        P(None, "ty", "tx"),
        P(None, "ty", "tx"),
    )
    out_specs = (P(None, "ty", "tx"), P(None, "ty", "tx"), P(None, "ty", "tx"))
    return jax.shard_map(body, mesh=mesh, in_specs=in_specs, out_specs=out_specs, check_vma=False)
```

```python
import functools

import jax
import jax.numpy as jnp
from jax import lax
from jax.experimental import pallas as pl
from jax.experimental.pallas import tpu as pltpu
from jax.sharding import PartitionSpec as P

PANELS = 4
STEPS = 4
TPATCH = 128
HALO = 4
SUB = 8
FIELDS = 3
COURANT = 0.15
GRADIENT = 0.3
CHUNKS = (2, 2, 2, 2)
PAIRS = ((0,), (1,), (2,), (3,))
GROUPS = ((0, 1, 2, 3),)
ORDER = "P0 P1 P2 J0 P3 J1 J2 S0 F0 J3 S1 F1 S2 F2 S3 F3 H0"
GROUP = 16
VMEM = 61 * 2**20

ROWS_BY_ROWS = (((1,), (1,)), ((), ()))


def params(limit=VMEM):
    return pltpu.CompilerParams(vmem_limit_bytes=limit)


def in_vmem(count):
    return [pl.BlockSpec(memory_space=pltpu.VMEM)] * count


def in_smem(count):
    return [pl.BlockSpec(memory_space=pltpu.SMEM)] * count


def in_hbm(count):
    return [pl.BlockSpec(memory_space=pl.ANY)] * count


def spread(source, left, right):
    fields, levels, rows, width = source.shape
    half = width // 2
    for l in range(levels):
        for c in range(fields):
            at = pl.ds((l * fields + c) * rows, rows)
            left[at, :] = source[c, l, :, :half].astype(jnp.float32)
            right[at, :] = source[c, l, :, half:].astype(jnp.float32)


def row_block(left, right, s, count):
    at = pl.ds(s, count, stride=left.shape[0] // count)
    return jnp.concatenate([left[at, :], right[at, :]], axis=1).astype(jnp.bfloat16)


def write_out(cuts, fields, capacity, slots, outs, sems):
    count, copies = fields * cuts[0][-1], []
    starts = [(o * count + fields * first) * capacity for o, cut in enumerate(cuts) for first in cut[:-1]]
    for i, (start, out) in enumerate(zip(starts, outs)):
        copies.append(pltpu.make_async_copy(slots.at[pl.ds(start, out.shape[0])], out, sems.at[i]))
        copies[-1].start()
    for copy in copies:
        copy.wait()


def terms_kernel(cuts, group, capacity, offsets, increments, weights, *refs):
    fields, levels, rows, _ = increments.shape
    count, tops = fields * levels, offsets.shape[0]
    outs = refs[:-9]
    held, source, left, right, slots, used, source_sem, held_sem, out_sem = refs[-9:]
    groups = rows // group
    first = pltpu.make_async_copy(increments, source, source_sem)
    first.start()

    def fetch(g):
        piece = pl.ds(g * group, group)
        return pltpu.make_async_copy(weights.at[piece], held.at[piece], held_sem.at[g])

    @pl.loop(0, groups)
    def _(g):
        fetch(g).start()

    for o in range(len(cuts)):
        used[o] = 0
    slots[...] = jnp.zeros_like(slots)
    first.wait()
    spread(source, left, right)

    @pl.loop(0, groups)
    def _(g):
        fetch(g).wait()
        for j in range(group):
            s = g * group + j
            block = row_block(left, right, s, count)
            term = lax.dot_general(block, held[s], ROWS_BY_ROWS, preferred_element_type=jnp.float32)
            for t in range(tops):
                o = offsets[t, s]
                k = used[o]
                used[o] = k + 1
                at = pl.ds(o * (count * capacity) + k, count, stride=capacity)
                slots[at, :] = term[:, t * TPATCH : (t + 1) * TPATCH]

    write_out(cuts, fields, capacity, slots, outs, out_sem)


def terms(cuts, capacity, offsets, increments, weights):
    fields, levels, rows, width = increments.shape
    tops, wide = offsets.shape[0], weights.shape[-1]
    count = fields * levels
    group = max(g for g in range(1, GROUP + 1) if rows % g == 0)
    sizes = [last - first for cut in cuts for first, last in zip(cut[:-1], cut[1:])]
    weights = weights.reshape(rows, tops * TPATCH, wide)
    out = pl.pallas_call(
        functools.partial(terms_kernel, cuts, group, capacity),
        in_specs=in_smem(1) + in_hbm(2),
        out_specs=in_hbm(len(sizes)),
        out_shape=[jax.ShapeDtypeStruct((fields * size * capacity, TPATCH), jnp.float32) for size in sizes],
        scratch_shapes=[
            pltpu.VMEM(weights.shape, jnp.bfloat16),
            pltpu.VMEM(increments.shape, jnp.bfloat16),
            pltpu.VMEM((count * rows, width // 2), jnp.float32),
            pltpu.VMEM((count * rows, width // 2), jnp.float32),
            pltpu.VMEM((len(cuts) * count * capacity, TPATCH), jnp.float32),
            pltpu.SMEM((len(cuts),), jnp.int32),
            pltpu.SemaphoreType.DMA,
            pltpu.SemaphoreType.DMA((rows // group,)),
            pltpu.SemaphoreType.DMA((len(sizes),)),
        ],
        compiler_params=params(),
        cost_estimate=pl.CostEstimate(flops=0, bytes_accessed=rows * tops * TPATCH * wide * 2, transcendentals=0),
        name="terms",
    )(offsets, increments, weights)
    given = []
    for cut in cuts:
        given.append(out[: len(cut) - 1])
        out = out[len(cut) - 1 :]
    return given


def sum_kernel(which, parity, patches, odd, places, *refs):
    slot_arrays, refs = refs[: len(which)], refs[len(which) :]
    wholes, outs, partial = [], refs[:-1], refs[-1]
    if parity is not None:
        wholes, outs = outs[:1], outs[1:]
    count = sum(out.shape[0] for out in outs) // patches
    capacity = slot_arrays[0].shape[0] // count
    totals = [partial.at[i] for i in range(len(slot_arrays))]
    for held in totals:
        held[...] = jnp.zeros_like(held)

    def one(k, carry):
        for row, slots, held in zip(which, slot_arrays, totals):
            at = pl.ds(places[row, k], count, stride=patches)
            held[at, :] = held[at, :] + slots[pl.ds(k, count, stride=capacity), :]
        return carry

    lax.fori_loop(0, capacity, one, 0, unroll=4)
    start = 0
    for out in outs:
        at = pl.ds(start, out.shape[0])
        total = totals[0][at, :]
        for more in totals[1:]:
            total = total + more[at, :]
        out[...] = total
        start += out.shape[0]
        if wholes:

            @pl.when(odd[0] == parity)
            def _():
                out[...] += wholes[0][at, :]


def patch_sums(odd, places, slot_arrays, which, patches, counts, whole=None, parity=None):
    wholes = [] if whole is None else [whole]
    return pl.pallas_call(
        functools.partial(sum_kernel, which, parity, patches),
        in_specs=in_smem(2) + in_vmem(len(wholes) + len(slot_arrays)),
        out_specs=in_vmem(len(counts)),
        out_shape=[jax.ShapeDtypeStruct((count * patches, TPATCH), jnp.float32) for count in counts],
        scratch_shapes=[pltpu.VMEM((len(slot_arrays), sum(counts) * patches, TPATCH), jnp.float32)],
        compiler_params=params(24 * 2**20),
        name="patch_sums",
    )(odd, places, *slot_arrays, *wholes)


def fields_kernel(first, settled, last, basis, thickness, wind_first, wind_second, *refs):
    depth, cov_first, cov_second, low_rows, high_rows, low_cols, high_cols = refs[-7:]
    rows, cols = depth.shape[1:]
    blocks = cols // TPATCH
    patches = rows * blocks
    lane = lax.broadcasted_iota(jnp.int32, (rows, TPATCH), 1)

    @pl.when(pl.program_id(0) == 0)
    def _():
        if first:
            low_cols[...] = refs[0][...]
            high_cols[...] = refs[1][...]
        else:
            low, high = (jnp.zeros((rows, TPATCH), jnp.float32) for _ in range(2))
            for f in range(FIELDS):
                lanes = TPATCH - (FIELDS - f) * HALO
                here = (lane >= lanes) & (lane < lanes + HALO)
                tile = refs[1][...] if f == FIELDS - 1 else refs[0][f]
                low = jnp.where(here, pltpu.roll(tile[:, :TPATCH], lanes, 1), low)
                high = jnp.where(here, pltpu.roll(tile[:, cols - TPATCH :], (lanes + HALO) % TPATCH, 1), high)
            low_cols[...] = low
            high_cols[...] = high

    for block in range(blocks):
        at = slice(block * TPATCH, (block + 1) * TPATCH)
        pieces = [slice(c * patches + block * rows, c * patches + (block + 1) * rows) for c in range(FIELDS)]
        east, north, thick = (settled[piece, :] + last[piece, :] for piece in pieces)
        values = (
            thickness[0, :, at] + thick,
            wind_first[0, :, at] + basis[0, :, at] * east + basis[1, :, at] * north,
            wind_second[0, :, at] + basis[2, :, at] * east + basis[3, :, at] * north,
        )
        for f, (ref, value) in enumerate(zip((depth, cov_first, cov_second), values)):
            ref[0, :, at] = value
            low_rows[0, f, :, at] = value[:HALO]
            high_rows[0, f, :, at] = value[rows - HALO :]
            lanes = ((first + pl.program_id(0)) * FIELDS + f) * HALO
            here = (lane >= lanes) & (lane < lanes + HALO)
            if block == 0:
                low_cols[...] = jnp.where(here, pltpu.roll(value, lanes, 1), low_cols[...])
            if block == blocks - 1:
                high_cols[...] = jnp.where(here, pltpu.roll(value, lanes + HALO, 1), high_cols[...])


def first_fields(begin, first, levels, total, patches, settled, last, basis, thickness, wind_first, wind_second, metric, sides, so_far):
    rows, cols = thickness.shape[1:]
    fixed = lambda shape: pl.BlockSpec(shape, lambda l: (0,) * len(shape))
    of_level = lambda start: pl.BlockSpec((1, rows, cols), lambda l: (start + l, 0, 0))
    of_ends = pl.BlockSpec((1, FIELDS, HALO, cols), lambda l: (first - begin + l, 0, 0, 0))
    of_patches = pl.BlockSpec((FIELDS * patches, TPATCH), lambda l: (l, 0))
    shapes = [(total, rows, cols)] * 3 + [(total + 2, FIELDS, HALO, cols)] * 2 + [(rows, TPATCH)] * 2
    beside = sides if so_far else metric
    out = pl.pallas_call(
        functools.partial(fields_kernel, first - begin),
        grid=(levels,),
        in_specs=[of_patches, of_patches, fixed(basis.shape)]
        + [of_level(first)] * 3
        + [fixed(array.shape) for array in beside]
        + in_hbm(len(so_far)),
        out_specs=[of_level(first - begin)] * 3 + [of_ends] * 2 + [fixed((rows, TPATCH))] * 2,
        out_shape=[jax.ShapeDtypeStruct(shape, jnp.float32) for shape in shapes],
        input_output_aliases={8 + i: i for i in range(len(so_far))},
        compiler_params=params(32 * 2**20),
        name="first_fields",
    )(settled, last, basis, thickness, wind_first, wind_second, *beside, *so_far)
    return out[:5], out[5:]


def with_rim(core, entry, lanes, from_below, from_above, left, right):
    ends = jnp.concatenate([from_above[entry], from_below[entry]], axis=0)
    lane = lax.broadcasted_iota(jnp.int32, left.shape, 1)
    rim = jnp.where(
        lane < HALO,
        pltpu.roll(right, (TPATCH - lanes) % TPATCH, 1),
        jnp.where(lane >= TPATCH - HALO, pltpu.roll(left, TPATCH - HALO - lanes, 1), 0.0),
    )
    return jnp.concatenate([jnp.concatenate([core, ends], axis=0), rim], axis=1)


def columns(own, from_below, from_above, side):
    entry = (from_below.shape[0] - 1, side)
    return jnp.concatenate(
        [own[...], from_above[*entry, :, :TPATCH], from_below[*entry, :, :TPATCH]], axis=0
    )


def steps_kernel(diag, cross, turns, wall, *refs):
    metric_halos, halos = refs[:4], refs[4:8]
    parts, outs, rimmed = refs[8 : 8 + FIELDS], refs[-FIELDS - 1 : -1], refs[-1]
    rows, cols = parts[0].shape[1:]
    ext_cols = cols + TPATCH
    l = pl.program_id(0)

    @pl.when(l == 0)
    def _():
        below, above, *own = metric_halos
        left, right = (columns(own[side], below, above, side) for side in range(2))
        for f in range(FIELDS):
            tile = cross[...] if f == FIELDS - 1 else diag[f]
            entry, lanes = (below.shape[0] - 2, f), TPATCH - (FIELDS - f) * HALO
            rimmed[f] = with_rim(tile, entry, lanes, below, above, left, right)

    below, above, *own = halos
    left, right = (columns(own[side], below, above, side) for side in range(2))
    depth, cov_first, cov_second = (
        with_rim(parts[f][0], (l, f), (l * FIELDS + f) * HALO, below, above, left, right) for f in range(FIELDS)
    )
    cos_below, sin_below, cos_above, sin_above = (
        jnp.concatenate([turns[i]] * (ext_cols // TPATCH), axis=1) for i in range(4)
    )
    before = lambda v, axis: pltpu.roll(v, 1, axis)
    after = lambda v, axis: pltpu.roll(v, v.shape[axis] - 1, axis)
    for _ in range(STEPS):
        con_first = rimmed[0] * cov_first + rimmed[2] * cov_second
        con_second = rimmed[2] * cov_first + rimmed[1] * cov_second
        depth_below, depth_above = before(depth, 0), after(depth, 0)
        second_below = sin_below * before(con_first, 0) + cos_below * before(con_second, 0)
        second_above = sin_above * after(con_first, 0) + cos_above * after(con_second, 0)
        face_below = 0.5 * (con_second + second_below)
        flux_below = jnp.maximum(face_below, 0.0) * depth_below + jnp.minimum(face_below, 0.0) * depth
        face_above = 0.5 * (con_second + second_above)
        flux_above = jnp.maximum(face_above, 0.0) * depth + jnp.minimum(face_above, 0.0) * depth_above
        depth_left, depth_right = before(depth, 1), after(depth, 1)
        face_left = 0.5 * (con_first + before(con_first, 1)) * wall[0:1, :]
        flux_left = jnp.maximum(face_left, 0.0) * depth_left + jnp.minimum(face_left, 0.0) * depth
        flux_right = after(flux_left, 1)
        depth = depth - COURANT * ((flux_right - flux_left) + (flux_above - flux_below))
        cov_first = cov_first - GRADIENT * 0.5 * (depth_right - depth_left)
        cov_second = cov_second - GRADIENT * 0.5 * (depth_above - depth_below)
    for ref, value in zip(outs, (depth, cov_first, cov_second)):
        ref[0] = value[:rows, :cols]


def steps(first, levels, total, diag, cross, turns, wall, metric_halos, halos, parts, so_far):
    rows, cols = parts[0].shape[1:]
    fixed = lambda array: pl.BlockSpec(array.shape, lambda l: (0,) * array.ndim)
    of_level = lambda start: pl.BlockSpec((1, rows, cols), lambda l: (start + l, 0, 0))
    given = (diag, cross, turns, wall, *metric_halos, *halos)
    return pl.pallas_call(
        steps_kernel,
        grid=(levels,),
        in_specs=[fixed(array) for array in given] + [of_level(0)] * FIELDS + in_hbm(len(so_far)),
        out_specs=[of_level(first)] * FIELDS,
        out_shape=[jax.ShapeDtypeStruct((total, rows, cols), jnp.float32)] * FIELDS,
        input_output_aliases={len(given) + FIELDS + i: i for i in range(len(so_far))},
        scratch_shapes=[pltpu.VMEM((FIELDS, rows + SUB, cols + TPATCH), jnp.float32)],
        compiler_params=params(32 * 2**20),
        cost_estimate=pl.CostEstimate(flops=0, bytes_accessed=levels * 4 * 2**20, transcendentals=0),
        name="steps",
    )(*given, *parts, *so_far)


def quarter_turn(code):
    cosine = (code == 0).astype(jnp.float32) - (code == 2).astype(jnp.float32)
    sine_value = (code == 1).astype(jnp.float32) - (code == 3).astype(jnp.float32)
    return (cosine, sine_value)


def turn_factors(first_row, rows, total_rows, rotation):
    index = jnp.arange(rows + SUB, dtype=jnp.int32)
    index = jnp.where(index < rows + HALO, index, index - rows - SUB)
    row = (first_row + index) % total_rows
    panel_rows = total_rows // PANELS
    matches = jnp.arange(PANELS, dtype=jnp.int32)[None, :] == (row // panel_rows)[:, None]
    lower = jnp.sum(jnp.where(matches, rotation[0][None, :], 0), axis=1)
    upper = jnp.sum(jnp.where(matches, rotation[1][None, :], 0), axis=1)
    below = jnp.where(row % panel_rows == 0, lower, 0)
    above = jnp.where(row % panel_rows == panel_rows - 1, upper, 0)
    factors = jnp.stack(quarter_turn(below) + quarter_turn(above))
    return jnp.broadcast_to(factors[:, :, None], factors.shape + (TPATCH,))


def shift(array, axis, by, closed):
    size = lax.axis_size(axis)
    pairs = [(i, (i + by) % size) for i in range(size) if closed or 0 <= i + by < size]
    return lax.ppermute(array, axis, pairs)


def together(*arrays):
    return lax.optimization_barrier(arrays)


def body(
    increments,
    remap_weights,
    dest_offset,
    slot_patch,
    rotation,
    basis,
    inv_metric_diag,
    inv_metric_cross,
    thickness,
    wind_first,
    wind_second,
):
    levels, rows, cols = thickness.shape
    tx_count, ty_count = lax.axis_size("tx"), lax.axis_size("ty")
    tx_index, ty_index = lax.axis_index("tx"), lax.axis_index("ty")
    owners, capacity = slot_patch.shape[2:]
    blocks = cols // TPATCH
    patches = rows * blocks
    bounds = [0]
    while bounds[-1] < levels:
        bounds.append(min(levels, bounds[-1] + CHUNKS[len(bounds) - 1]))
    parts = len(bounds) - 1

    evens, odds = range(0, ty_count, 2), range(1, ty_count, 2)
    swap = [(b, b + 1) for b in evens] + [(b, b - 1) for b in odds]
    send = lambda array, pairs: lax.ppermute(array, "ty", pairs)

    to_next = [(b, (b + 2) % ty_count) for b in range(ty_count)]
    places_of = [slot_patch[0, 0]] + [shift(slot_patch[0, 0], "ty", -by, True) for by in (1, 2)]
    odd = (ty_index % 2).reshape(1)

    offsets = dest_offset[0, 0].T
    counts = [FIELDS * (last - first) for first, last in zip(bounds[:-1], bounds[1:])]
    wide = [bounds[pair[0]] for pair in PAIRS] + [levels]
    cuts = [bounds, wide] + [bounds] * (owners - 3) + [wide]
    own, first, second, far = terms(cuts, capacity, offsets, increments, remap_weights)
    *far, places_of[1], places_of[2] = together(*far, places_of[1], places_of[2])
    places, places_next, places_second = ((p % blocks) * rows + p // blocks for p in places_of)
    turns = turn_factors(ty_index * rows, rows, rows * ty_count, rotation)
    column = jnp.arange(cols + TPATCH, dtype=jnp.int32)
    column = tx_index * cols + jnp.where(column < cols + TPATCH // 2, column, column - cols - TPATCH)
    wall = jnp.where((column == 0) | (column == cols * tx_count), 0.0, 1.0).astype(jnp.float32)
    wall = jnp.broadcast_to(wall[None, :], (SUB, cols + TPATCH))

    thirds = [send(slots, to_next) for slots in far]
    token, payload = odd, None
    across, last, settled, found, edges, pending = {}, {}, {}, {}, {}, []
    for step in ORDER.split():
        kind, n = step[0], int(step[1:])
        if kind == "P":
            chunks = PAIRS[n]
            paired = patch_sums(token, places_next, [thirds[n], first[n]], (3, 1), patches, [counts[j] for j in chunks])
            token, *paired = together(token, *paired)
            for j, part in zip(chunks, paired):
                across[j] = send(part, swap)
            if n == 0:
                token, turns, wall = together(token, turns, wall)
        elif kind == "J":
            (joined,) = patch_sums(token, places_second, [second[n]], (2,), patches, [counts[n]], across[n], 0)
            token, joined = together(token, joined)
            last[n] = send(joined, to_next)
        elif kind == "S":
            (settled[n],) = patch_sums(token, places, [own[n]], (0,), patches, [counts[n]], across[n], 1)
            token, settled[n] = together(token, settled[n])
        elif kind == "F":
            (g,) = (i for i, group in enumerate(GROUPS) if n in group)
            begin, total = bounds[GROUPS[g][0]], bounds[GROUPS[g][-1] + 1] - bounds[GROUPS[g][0]]
            token, ready = together(token, settled[n])
            found[g], edges[g] = first_fields(
                begin, bounds[n], bounds[n + 1] - bounds[n], total, patches, ready, last[n], basis, thickness,
                wind_first, wind_second, (inv_metric_diag, inv_metric_cross), edges.get(g), found.get(g, []),
            )
            token, *edges[g] = together(token, *edges[g])
        else:
            begin, total = bounds[GROUPS[n][0]], bounds[GROUPS[n][-1] + 1] - bounds[GROUPS[n][0]]
            *fields, low_rows, high_rows = found[n]
            low_cols, high_cols = edges[n]
            from_left = shift(high_cols, "tx", 1, False)
            from_right = shift(low_cols, "tx", -1, False)

            def ends(entries, at):
                metric = jnp.concatenate([inv_metric_diag, inv_metric_cross[None]], axis=0)[:, at : at + HALO]
                corners = jnp.stack([side[at : at + HALO] for side in (from_left, from_right)])
                corners = jnp.pad(corners, ((0, FIELDS - 2), (0, 0), (0, cols - TPATCH)))
                return entries.at[total].set(metric).at[total + 1].set(corners)

            payload = (ends(high_rows, rows - HALO), ends(low_rows, 0))
            halos = (shift(payload[0], "ty", 1, True), shift(payload[1], "ty", -1, True), from_left, from_right)
            token, *halos = together(token, *halos)
            pending.append((begin, total, halos, fields))

    results, metric_halos = [], pending[0][2]
    for n, (begin, total, halos, fields) in enumerate(pending):
        results = steps(
            begin, total, levels, inv_metric_diag, inv_metric_cross, turns, wall, metric_halos, halos, fields, results
        )
    return tuple(results)


def solution(mesh):
    in_specs = (
        P(None, None, "tx", "ty"),
        P("tx", "ty", None, None, None, None),
        P("tx", "ty", None, None),
        P("tx", "ty", None, None),
        P(),
        P(None, "ty", "tx"),
        P(None, "ty", "tx"),
        P("ty", "tx"),
        P(None, "ty", "tx"),
        P(None, "ty", "tx"),
        P(None, "ty", "tx"),
    )
    out_specs = (P(None, "ty", "tx"), P(None, "ty", "tx"), P(None, "ty", "tx"))
    return jax.shard_map(body, mesh=mesh, in_specs=in_specs, out_specs=out_specs, check_vma=False)
```

```python
import functools

import jax
import jax.numpy as jnp
from jax import lax
from jax.experimental import pallas as pl
from jax.experimental.pallas import tpu as pltpu
from jax.sharding import PartitionSpec as P

PANELS = 4
STEPS = 4
TPATCH = 128
HALO = 4
SUB = 8
FIELDS = 3
COURANT = 0.15
GRADIENT = 0.3
GRADIENT_HALF = GRADIENT * 0.5
CHUNKS = (2, 2, 2, 2)
PAIRS = ((0,), (1,), (2,), (3,))
GROUPS = ((0, 1), (2, 3))
LATE = ()
EARLY = ((0, 2),)
ORDER = (
    "P0", "P1", "P2", "J0", "P3", "J1", "S0", "S1", "J2", "F0", "J3", "S2", "S3", "F1", "F2", "H0", "F3", "H1",
)
GROUP = 16
VMEM = 61 * 2**20

ROWS_BY_ROWS = (((1,), (1,)), ((), ()))


def params(limit=VMEM):
    return pltpu.CompilerParams(vmem_limit_bytes=limit)


def in_vmem(count):
    return [pl.BlockSpec(memory_space=pltpu.VMEM)] * count


def in_smem(count):
    return [pl.BlockSpec(memory_space=pltpu.SMEM)] * count


def in_hbm(count):
    return [pl.BlockSpec(memory_space=pl.ANY)] * count


def spread(source, left, right):
    fields, levels, rows, width = source.shape
    half = width // 2
    for l in range(levels):
        for c in range(fields):
            at = pl.ds((l * fields + c) * rows, rows)
            left[at, :] = source[c, l, :, :half].astype(jnp.float32)
            right[at, :] = source[c, l, :, half:].astype(jnp.float32)


def row_block(left, right, s, count):
    at = pl.ds(s, count, stride=left.shape[0] // count)
    return jnp.concatenate([left[at, :], right[at, :]], axis=1).astype(jnp.bfloat16)


def write_out(cuts, fields, capacity, slots, outs, sems):
    count, copies = fields * cuts[0][-1], []
    starts = [(o * count + fields * first) * capacity for o, cut in enumerate(cuts) for first in cut[:-1]]
    for i, (start, out) in enumerate(zip(starts, outs)):
        copies.append(pltpu.make_async_copy(slots.at[pl.ds(start, out.shape[0])], out, sems.at[i]))
        copies[-1].start()
    for copy in copies:
        copy.wait()


def terms_kernel(cuts, group, capacity, offsets, increments, weights, *refs):
    fields, levels, rows, _ = increments.shape
    count, tops = fields * levels, offsets.shape[0]
    outs = refs[:-9]
    held, source, left, right, slots, used, source_sem, held_sem, out_sem = refs[-9:]
    groups = rows // group
    first = pltpu.make_async_copy(increments, source, source_sem)
    first.start()

    def fetch(g):
        piece = pl.ds(g * group, group)
        return pltpu.make_async_copy(weights.at[piece], held.at[piece], held_sem.at[g])

    @pl.loop(0, groups)
    def _(g):
        fetch(g).start()

    for o in range(len(cuts)):
        used[o] = 0
    slots[...] = jnp.zeros_like(slots)
    first.wait()
    spread(source, left, right)

    @pl.loop(0, groups)
    def _(g):
        fetch(g).wait()
        for j in range(group):
            s = g * group + j
            block = row_block(left, right, s, count)
            term = lax.dot_general(block, held[s], ROWS_BY_ROWS, preferred_element_type=jnp.float32)
            for t in range(tops):
                o = offsets[t, s]
                k = used[o]
                used[o] = k + 1
                at = pl.ds(o * (count * capacity) + k, count, stride=capacity)
                slots[at, :] = term[:, t * TPATCH : (t + 1) * TPATCH]

    write_out(cuts, fields, capacity, slots, outs, out_sem)


def terms(cuts, capacity, offsets, increments, weights):
    fields, levels, rows, width = increments.shape
    tops, wide = offsets.shape[0], weights.shape[-1]
    count = fields * levels
    group = max(g for g in range(1, GROUP + 1) if rows % g == 0)
    sizes = [last - first for cut in cuts for first, last in zip(cut[:-1], cut[1:])]
    weights = weights.reshape(rows, tops * TPATCH, wide)
    out = pl.pallas_call(
        functools.partial(terms_kernel, cuts, group, capacity),
        in_specs=in_smem(1) + in_hbm(2),
        out_specs=in_hbm(len(sizes)),
        out_shape=[jax.ShapeDtypeStruct((fields * size * capacity, TPATCH), jnp.float32) for size in sizes],
        scratch_shapes=[
            pltpu.VMEM(weights.shape, jnp.bfloat16),
            pltpu.VMEM(increments.shape, jnp.bfloat16),
            pltpu.VMEM((count * rows, width // 2), jnp.float32),
            pltpu.VMEM((count * rows, width // 2), jnp.float32),
            pltpu.VMEM((len(cuts) * count * capacity, TPATCH), jnp.float32),
            pltpu.SMEM((len(cuts),), jnp.int32),
            pltpu.SemaphoreType.DMA,
            pltpu.SemaphoreType.DMA((rows // group,)),
            pltpu.SemaphoreType.DMA((len(sizes),)),
        ],
        compiler_params=params(),
        cost_estimate=pl.CostEstimate(flops=0, bytes_accessed=rows * tops * TPATCH * wide * 2, transcendentals=0),
        name="terms",
    )(offsets, increments, weights)
    given = []
    for cut in cuts:
        given.append(out[: len(cut) - 1])
        out = out[len(cut) - 1 :]
    return given


def sum_kernel(which, parity, patches, odd, places, *refs):
    slot_arrays, refs = refs[: len(which)], refs[len(which) :]
    wholes, outs, partial = [], refs[:-1], refs[-1]
    if parity is not None:
        wholes, outs = outs[:1], outs[1:]
    count = sum(out.shape[0] for out in outs) // patches
    capacity = slot_arrays[0].shape[0] // count
    totals = [partial.at[i] for i in range(len(slot_arrays))]
    for held in totals:
        held[...] = jnp.zeros_like(held)

    def one(k, carry):
        for row, slots, held in zip(which, slot_arrays, totals):
            at = pl.ds(places[row, k], count, stride=patches)
            held[at, :] = held[at, :] + slots[pl.ds(k, count, stride=capacity), :]
        return carry

    lax.fori_loop(0, capacity, one, 0, unroll=4)
    start = 0
    for out in outs:
        at = pl.ds(start, out.shape[0])
        total = totals[0][at, :]
        for more in totals[1:]:
            total = total + more[at, :]
        out[...] = total
        start += out.shape[0]
        if wholes:

            @pl.when(odd[0] == parity)
            def _():
                out[...] += wholes[0][at, :]


def patch_sums(odd, places, slot_arrays, which, patches, counts, whole=None, parity=None):
    wholes = [] if whole is None else [whole]
    return pl.pallas_call(
        functools.partial(sum_kernel, which, parity, patches),
        in_specs=in_smem(2) + in_vmem(len(wholes) + len(slot_arrays)),
        out_specs=in_vmem(len(counts)),
        out_shape=[jax.ShapeDtypeStruct((count * patches, TPATCH), jnp.float32) for count in counts],
        scratch_shapes=[pltpu.VMEM((len(slot_arrays), sum(counts) * patches, TPATCH), jnp.float32)],
        compiler_params=params(24 * 2**20),
        name="patch_sums",
    )(odd, places, *slot_arrays, *wholes)


def fields_kernel(first, settled, last, basis, thickness, wind_first, wind_second, *refs):
    depth, cov_first, cov_second, low_rows, high_rows, low_cols, high_cols = refs[-7:]
    rows, cols = depth.shape[1:]
    blocks = cols // TPATCH
    patches = rows * blocks
    lane = lax.broadcasted_iota(jnp.int32, (rows, TPATCH), 1)

    @pl.when(pl.program_id(0) == 0)
    def _():
        if first:
            low_cols[...] = refs[0][...]
            high_cols[...] = refs[1][...]
        else:
            low, high = (jnp.zeros((rows, TPATCH), jnp.float32) for _ in range(2))
            for f in range(FIELDS):
                lanes = TPATCH - (FIELDS - f) * HALO
                here = (lane >= lanes) & (lane < lanes + HALO)
                tile = refs[1][...] if f == FIELDS - 1 else refs[0][f]
                low = jnp.where(here, pltpu.roll(tile[:, :TPATCH], lanes, 1), low)
                high = jnp.where(here, pltpu.roll(tile[:, cols - TPATCH :], (lanes + HALO) % TPATCH, 1), high)
            low_cols[...] = low
            high_cols[...] = high

    for block in range(blocks):
        at = slice(block * TPATCH, (block + 1) * TPATCH)
        pieces = [slice(c * patches + block * rows, c * patches + (block + 1) * rows) for c in range(FIELDS)]
        east, north, thick = (settled[piece, :] + last[piece, :] for piece in pieces)
        values = (
            thickness[0, :, at] + thick,
            wind_first[0, :, at] + basis[0, :, at] * east + basis[1, :, at] * north,
            wind_second[0, :, at] + basis[2, :, at] * east + basis[3, :, at] * north,
        )
        for f, (ref, value) in enumerate(zip((depth, cov_first, cov_second), values)):
            ref[0, :, at] = value
            low_rows[f, :, at] = value[:HALO]
            high_rows[f, :, at] = value[rows - HALO :]
            lanes = ((first + pl.program_id(0)) * FIELDS + f) * HALO
            here = (lane >= lanes) & (lane < lanes + HALO)
            if block == 0:
                low_cols[...] = jnp.where(here, pltpu.roll(value, lanes, 1), low_cols[...])
            if block == blocks - 1:
                high_cols[...] = jnp.where(here, pltpu.roll(value, lanes + HALO, 1), high_cols[...])


def first_fields(place, levels, patches, settled, last, basis, thickness, wind_first, wind_second, metric, sides, fields, ends, later):
    first, begin, total, extra = place
    every, rows, cols = thickness.shape
    fixed = lambda shape: pl.BlockSpec(shape, lambda l: (0,) * len(shape))
    of_level = pl.BlockSpec((1, rows, cols), lambda l: (first + l, 0, 0))
    of_ends = pl.BlockSpec((FIELDS, HALO, cols), lambda l: (first - begin + l, 0, 0))
    of_patches = pl.BlockSpec((FIELDS * patches, TPATCH), lambda l: (l, 0))
    shapes = [(every, rows, cols)] * 3 + [(total * FIELDS + extra, HALO, cols)] * 2 + [(rows, TPATCH)] * 2
    beside = sides if ends else metric
    given = [*fields, *ends]
    aliases = {8 + i: i for i in range(len(fields))}
    aliases.update({8 + len(fields) + i: FIELDS + i for i in range(len(ends))})
    out = pl.pallas_call(
        functools.partial(fields_kernel, first - begin),
        grid=(levels,),
        in_specs=[of_patches, of_patches, fixed(basis.shape)]
        + [of_level] * 3
        + [fixed(array.shape) for array in beside]
        + in_hbm(len(given) + len(later)),
        out_specs=[of_level] * 3 + [of_ends] * 2 + [fixed((rows, TPATCH))] * 2,
        out_shape=[jax.ShapeDtypeStruct(shape, jnp.float32) for shape in shapes],
        input_output_aliases=aliases,
        compiler_params=params(32 * 2**20),
        name="first_fields",
    )(settled, last, basis, thickness, wind_first, wind_second, *beside, *given, *later)
    return out[:3], out[3:5], out[5:]


def entries_kernel(diag, cross, left, right, *refs):
    outs, i, count = refs[-2:], pl.program_id(0), pl.num_programs(0)
    rows, cols = cross.shape
    for out, at in zip(outs, (0, rows - HALO)):
        for f in range(FIELDS):

            @pl.when((i == f) & (i < count - 1))
            def _():
                out[0] = cross[at : at + HALO, :] if f == FIELDS - 1 else diag[f, at : at + HALO, :]

        @pl.when(i == count - 1)
        def _():
            out[...] = jnp.zeros_like(out)
            out[0, :, :TPATCH] = left[at : at + HALO, :]
            out[0, :, TPATCH : 2 * TPATCH] = right[at : at + HALO, :]


def last_entries(extra, ends, diag, cross, sides, later):
    whole, cols = ends[0].shape[0], ends[0].shape[-1]
    entry = pl.BlockSpec((1, HALO, cols), lambda i: (whole - extra + i, 0, 0))
    fixed = lambda array: pl.BlockSpec(array.shape, lambda i: (0,) * array.ndim)
    given = (diag, cross, *sides)
    return pl.pallas_call(
        entries_kernel,
        grid=(extra,),
        in_specs=[fixed(array) for array in given] + in_hbm(len(ends) + len(later)),
        out_specs=[entry] * 2,
        out_shape=[jax.ShapeDtypeStruct(end.shape, jnp.float32) for end in ends],
        input_output_aliases={len(given) + i: i for i in range(len(ends))},
        compiler_params=params(16 * 2**20),
        name="last_entries",
    )(*given, *ends, *later)


def rim_tile(lanes, left, right):
    lane = lax.broadcasted_iota(jnp.int32, left.shape, 1)
    return jnp.where(
        lane < HALO,
        pltpu.roll(right, (TPATCH - lanes) % TPATCH, 1),
        jnp.where(lane >= TPATCH - HALO, pltpu.roll(left, TPATCH - HALO - lanes, 1), 0.0),
    )


def upwind(face, behind, ahead):
    return face * jnp.where(face > 0.0, behind, ahead)


def steps_kernel(skipped, total_rows, spot, rotation, diag, cross, *refs):
    metric_halos, halos, parts = refs[:4], refs[4:8], refs[8 : 8 + FIELDS]
    outs, done, rimmed, wall = refs[-FIELDS - 3 : -3], refs[-3], refs[-2], refs[-1]
    done[...] = jnp.zeros_like(done)
    rows, cols = parts[0].shape[1:]
    ext_rows, ext_cols = rows + SUB, cols + TPATCH
    panel_rows = total_rows // PANELS
    l = skipped + pl.program_id(0)

    def columns(below, above, *sides):
        last = below.shape[0] - 1
        corners = lambda n: [end[last, :, n * TPATCH : (n + 1) * TPATCH] for end in (above, below)]
        return [jnp.concatenate([side[...]] + corners(n), axis=0) for n, side in enumerate(sides)]

    def with_rim(core, above, below, lanes, sides):
        return jnp.concatenate([jnp.concatenate([core, above, below], axis=0), rim_tile(lanes, *sides)], axis=1)

    @pl.when(pl.program_id(0) == 0)
    def _():
        below, above = metric_halos[:2]
        sides, entry = columns(*metric_halos), below.shape[0] - 1 - FIELDS
        for f in range(FIELDS):
            core = cross[...] if f == FIELDS - 1 else diag[f]
            lanes = TPATCH - (FIELDS - f) * HALO
            rimmed[f] = with_rim(core, above[entry + f], below[entry + f], lanes, sides) * (COURANT * 0.5)
        column = lax.broadcasted_iota(jnp.int32, wall.shape, 1)
        walled = ((spot[2] == 0) & (column == 0)) | ((spot[2] == spot[3] - 1) & (column == cols))
        wall[...] = jnp.where(walled, 0.0, 1.0)

    turns = []
    for edge in (0, rows):
        upper = lax.rem(spot[1] * rows + edge, total_rows)
        lower = lax.rem(upper + total_rows - 1, total_rows)
        joint = lax.rem(upper, panel_rows) == 0
        codes = [rotation[0, upper // panel_rows], rotation[1, lower // panel_rows]]
        turns.append([factor for code in codes for factor in quarter_turn(jnp.where(joint, code, 0))])

    sides = columns(*halos)
    depth, cov_first, cov_second = (
        with_rim(
            parts[f][0], halos[1][l * FIELDS + f], halos[0][l * FIELDS + f], (l * FIELDS + f) * HALO, sides
        )
        for f in range(FIELDS)
    )
    before = lambda v, axis: pltpu.roll(v, 1, axis)
    after = lambda v, axis: pltpu.roll(v, v.shape[axis] - 1, axis)
    piece = lambda v, start: v[start : start + SUB]
    joints = ((0, rows, 0), (rows, rows - SUB, 1)), ((rows - SUB, rows, 1), (rows, 0, 0))
    depth = depth * GRADIENT_HALF
    for _ in range(STEPS):
        con_first = rimmed[0] * cov_first + rimmed[2] * cov_second
        con_second = rimmed[2] * cov_first + rimmed[1] * cov_second
        depth_below, depth_above = before(depth, 0), after(depth, 0)
        second_below = before(con_second, 0)
        second_above = after(con_second, 0)
        row = lax.broadcasted_iota(jnp.int32, (SUB, ext_cols), 0)
        below, above = [], []
        for at, source, joint in joints[0]:
            turned = turns[joint][0] * piece(second_below, at) + turns[joint][1] * before(piece(con_first, source), 0)
            below.append(jnp.where(row == 0, turned, piece(second_below, at)))
        second_below = jnp.concatenate([below[0], second_below[SUB:rows], below[1]], axis=0)
        flux_below = upwind(con_second + second_below, depth_below, depth)
        for at, source, joint in joints[1]:
            turned = turns[joint][2] * piece(second_above, at) + turns[joint][3] * after(piece(con_first, source), 0)
            second = jnp.where(row == SUB - 1, turned, piece(second_above, at))
            above.append(upwind(piece(con_second, at) + second, piece(depth, at), piece(depth_above, at)))
        flux_above = jnp.concatenate([after(flux_below, 0)[: rows - SUB]] + above, axis=0)
        depth_left, depth_right = before(depth, 1), after(depth, 1)
        flux_left = upwind((con_first + before(con_first, 1)) * wall[0:1, :], depth_left, depth)
        flux_right = after(flux_left, 1)
        cov_first = cov_first - (depth_right - depth_left)
        cov_second = cov_second - (depth_above - depth_below)
        depth = depth - ((flux_right - flux_left) + (flux_above - flux_below))
    for ref, value in zip(outs, (depth * (1.0 / GRADIENT_HALF), cov_first, cov_second)):
        ref[0] = value[:rows, :cols]


def steps(first, count, skipped, total_rows, spot, rotation, diag, cross, metric_halos, halos, parts, so_far):
    levels, rows, cols = parts[0].shape
    assert total_rows // PANELS % rows == 0
    fixed = lambda array: pl.BlockSpec(array.shape, lambda l: (0,) * array.ndim)
    of_level = pl.BlockSpec((1, rows, cols), lambda l: (first + l, 0, 0))
    given = (diag, cross, *metric_halos, *halos)
    before = 2 + len(given) + len(parts)
    return pl.pallas_call(
        functools.partial(steps_kernel, skipped, total_rows),
        grid=(count,),
        in_specs=in_smem(2) + [fixed(array) for array in given] + [of_level] * FIELDS + in_hbm(len(so_far)),
        out_specs=[of_level] * FIELDS + [pl.BlockSpec((SUB, TPATCH), lambda l: (0, 0))],
        out_shape=[jax.ShapeDtypeStruct((levels, rows, cols), jnp.float32)] * FIELDS
        + [jax.ShapeDtypeStruct((SUB, TPATCH), jnp.float32)],
        input_output_aliases={before + i: i for i in range(len(so_far))},
        scratch_shapes=[
            pltpu.VMEM((FIELDS, rows + SUB, cols + TPATCH), jnp.float32),
            pltpu.VMEM((SUB, cols + TPATCH), jnp.float32),
        ],
        compiler_params=params(32 * 2**20),
        name="steps",
    )(spot, rotation, *given, *parts, *so_far)


def quarter_turn(code):
    cosine = (code == 0).astype(jnp.float32) - (code == 2).astype(jnp.float32)
    sine_value = (code == 1).astype(jnp.float32) - (code == 3).astype(jnp.float32)
    return (cosine, sine_value)


def shift(array, axis, by, closed):
    size = lax.axis_size(axis)
    pairs = [(i, (i + by) % size) for i in range(size) if closed or 0 <= i + by < size]
    return lax.ppermute(array, axis, pairs)


def together(*arrays):
    return lax.optimization_barrier(arrays)


def body(
    increments,
    remap_weights,
    dest_offset,
    slot_patch,
    rotation,
    basis,
    inv_metric_diag,
    inv_metric_cross,
    thickness,
    wind_first,
    wind_second,
):
    levels, rows, cols = thickness.shape
    tx_count, ty_count = lax.axis_size("tx"), lax.axis_size("ty")
    tx_index, ty_index = lax.axis_index("tx"), lax.axis_index("ty")
    owners, capacity = slot_patch.shape[2:]
    blocks = cols // TPATCH
    patches = rows * blocks
    bounds = [0]
    while bounds[-1] < levels:
        bounds.append(min(levels, bounds[-1] + CHUNKS[len(bounds) - 1]))
    parts = len(bounds) - 1

    evens, odds = range(0, ty_count, 2), range(1, ty_count, 2)
    swap = [(b, b + 1) for b in evens] + [(b, b - 1) for b in odds]
    send = lambda array, pairs: lax.ppermute(array, "ty", pairs)

    to_next = [(b, (b + 2) % ty_count) for b in range(ty_count)]
    places = slot_patch.reshape(owners, capacity)
    places = (places % blocks) * rows + places // blocks
    ahead = [shift(slot_patch.reshape(owners, capacity), "ty", -by, True) for by in (1, 2)]
    spot = jnp.stack([ty_index % 2, ty_index, tx_index, jnp.int32(tx_count)])

    offsets = dest_offset.transpose(0, 1, 3, 2).reshape(-1, dest_offset.shape[2])
    counts = [FIELDS * (last - first) for first, last in zip(bounds[:-1], bounds[1:])]
    wide = [bounds[pair[0]] for pair in PAIRS] + [levels]
    cuts = [bounds, wide] + [bounds] * (owners - 3) + [wide]
    own, first, second, far = terms(cuts, capacity, offsets, increments, remap_weights)
    *far, ahead[0], ahead[1] = together(*far, *ahead)
    places_next, places_second = ((p % blocks) * rows + p // blocks for p in ahead)
    thirds = [send(slots, to_next) for slots in far]
    metric = (inv_metric_diag, inv_metric_cross)
    token, results, finished = spot, [], []

    def steps_on(n, first, count, results):
        skipped = first - bounds[GROUPS[n][0]]
        return steps(first, count, skipped, rows * ty_count, spot, rotation, *metric, halos[0], halos[n], fields, results)

    across, last, settled, ends, sides, fields, halos = {}, {}, {}, {}, {}, [], []
    for step in ORDER:
        kind, n = step[0], int(step[1:])
        if kind == "P":
            chunks = PAIRS[n]
            paired = patch_sums(token, places_next, [thirds[n], first[n]], (3, 1), patches, [counts[j] for j in chunks])
            token, *paired = together(token, *paired)
            for j, part in zip(chunks, paired):
                across[j] = send(part, swap)
        elif kind == "J":
            (joined,) = patch_sums(token, places_second, [second[n]], (2,), patches, [counts[n]], across[n], 0)
            token, joined = together(token, joined)
            last[n] = send(joined, to_next)
        elif kind == "S":
            (settled[n],) = patch_sums(token, places, [own[n]], (0,), patches, [counts[n]], across[n], 1)
            token, settled[n] = together(token, settled[n])
        elif kind == "F":
            (g,) = (i for i, group in enumerate(GROUPS) if n in group)
            begin = bounds[GROUPS[g][0]]
            place = (bounds[n], begin, bounds[GROUPS[g][-1] + 1] - begin, 1 if g else 1 + FIELDS)
            token, ready = together(token, settled[n])
            fields, ends[g], sides[g] = first_fields(
                place, bounds[n + 1] - bounds[n], patches, ready, last[n], basis, thickness, wind_first, wind_second,
                metric, sides.get(g), fields, ends.get(g, []),
                halos[0] if g and n in LATE else [],
            )
            token, *sides[g] = together(token, *sides[g])
        else:
            low_cols, high_cols = sides[n]
            beside = [shift(high_cols, "tx", 1, False), shift(low_cols, "tx", -1, False)]

            if n == len(GROUPS) - 1:
                for first, count in EARLY:
                    *results, finished = steps_on(0, first, count, results)
                    finished = [finished]
            high_rows, low_rows = reversed(last_entries(1 if n else 1 + FIELDS, ends[n], *metric, beside, finished))
            halos.append([shift(high_rows, "ty", 1, True), shift(low_rows, "ty", -1, True), *beside])

    done = EARLY[-1][0] + EARLY[-1][1] if EARLY else 0
    for n, group in enumerate(GROUPS):
        first, end = max(done, bounds[group[0]]), bounds[group[-1] + 1]
        *results, _ = steps_on(n, first, end - first, results)
    return tuple(results)


def solution(mesh):
    in_specs = (
        P(None, None, "tx", "ty"),
        P("tx", "ty", None, None, None, None),
        P("tx", "ty", None, None),
        P("tx", "ty", None, None),
        P(),
        P(None, "ty", "tx"),
        P(None, "ty", "tx"),
        P("ty", "tx"),
        P(None, "ty", "tx"),
        P(None, "ty", "tx"),
        P(None, "ty", "tx"),
    )
    out_specs = (P(None, "ty", "tx"), P(None, "ty", "tx"), P(None, "ty", "tx"))
    return jax.shard_map(body, mesh=mesh, in_specs=in_specs, out_specs=out_specs, check_vma=False)
```

```python
import functools

import jax
import jax.numpy as jnp
from jax import lax
from jax.experimental import pallas as pl
from jax.experimental.pallas import tpu as pltpu
from jax.sharding import PartitionSpec as P

PANELS = 4
STEPS = 4
TPATCH = 128
HALO = 4
SUB = 8
FIELDS = 3
COURANT = 0.15
GRADIENT = 0.3
GRADIENT_HALF = GRADIENT * 0.5
CHUNKS = (2, 2, 2, 2)
PAIRS = ((0,), (1,), (2,), (3,))
GROUPS = ((0, 1), (2, 3))
LATE = ()
EARLY = ((0, 2),)
ORDER = (
    "P0", "P1", "P2", "J0", "P3", "J1", "S0", "S1", "J2", "F0", "J3", "S2", "S3", "F1", "F2", "H0", "F3", "H1",
)
GROUP = 16
VMEM = 48 * 2**20

ROWS_BY_ROWS = (((1,), (1,)), ((), ()))


def params(limit=VMEM):
    return pltpu.CompilerParams(vmem_limit_bytes=limit)


def in_vmem(count):
    return [pl.BlockSpec(memory_space=pltpu.VMEM)] * count


def in_smem(count):
    return [pl.BlockSpec(memory_space=pltpu.SMEM)] * count


def in_hbm(count):
    return [pl.BlockSpec(memory_space=pl.ANY)] * count


def spread(source, left, right):
    fields, levels, rows, width = source.shape
    half = width // 2
    for l in range(levels):
        for c in range(fields):
            at = pl.ds((l * fields + c) * rows, rows)
            left[at, :] = source[c, l, :, :half].astype(jnp.float32)
            right[at, :] = source[c, l, :, half:].astype(jnp.float32)


def row_block(left, right, s, count):
    at = pl.ds(s, count, stride=left.shape[0] // count)
    return jnp.concatenate([left[at, :], right[at, :]], axis=1).astype(jnp.bfloat16)


def write_out(cuts, fields, capacity, slots, outs, sems):
    count, copies = fields * cuts[0][-1], []
    starts = [(o * count + fields * first) * capacity for o, cut in enumerate(cuts) for first in cut[:-1]]
    for i, (start, out) in enumerate(zip(starts, outs)):
        copies.append(pltpu.make_async_copy(slots.at[pl.ds(start, out.shape[0])], out, sems.at[i]))
        copies[-1].start()
    for copy in copies:
        copy.wait()


def terms_kernel(cuts, group, capacity, offsets, increments, weights, *refs):
    fields, levels, rows, _ = increments.shape
    count, tops = fields * levels, offsets.shape[0]
    outs = refs[:-9]
    held, source, left, right, slots, used, source_sem, held_sem, out_sem = refs[-9:]
    groups = rows // group
    first = pltpu.make_async_copy(increments, source, source_sem)
    first.start()

    def fetch(g):
        piece = pl.ds(g * group, group)
        return pltpu.make_async_copy(weights.at[piece], held.at[piece], held_sem.at[g])

    @pl.loop(0, groups)
    def _(g):
        fetch(g).start()

    for o in range(len(cuts)):
        used[o] = 0
    slots[...] = jnp.zeros_like(slots)
    first.wait()
    spread(source, left, right)

    @pl.loop(0, groups)
    def _(g):
        fetch(g).wait()
        for j in range(group):
            s = g * group + j
            block = row_block(left, right, s, count)
            term = lax.dot_general(block, held[s], ROWS_BY_ROWS, preferred_element_type=jnp.float32)
            for t in range(tops):
                o = offsets[t, s]
                k = used[o]
                used[o] = k + 1
                at = pl.ds(o * (count * capacity) + k, count, stride=capacity)
                slots[at, :] = term[:, t * TPATCH : (t + 1) * TPATCH]

    write_out(cuts, fields, capacity, slots, outs, out_sem)


def terms(cuts, capacity, offsets, increments, weights):
    fields, levels, rows, width = increments.shape
    tops, wide = offsets.shape[0], weights.shape[-1]
    count = fields * levels
    group = max(g for g in range(1, GROUP + 1) if rows % g == 0)
    sizes = [last - first for cut in cuts for first, last in zip(cut[:-1], cut[1:])]
    weights = weights.reshape(rows, tops * TPATCH, wide)
    out = pl.pallas_call(
        functools.partial(terms_kernel, cuts, group, capacity),
        in_specs=in_smem(1) + in_hbm(2),
        out_specs=in_hbm(len(sizes)),
        out_shape=[jax.ShapeDtypeStruct((fields * size * capacity, TPATCH), jnp.float32) for size in sizes],
        scratch_shapes=[
            pltpu.VMEM(weights.shape, jnp.bfloat16),
            pltpu.VMEM(increments.shape, jnp.bfloat16),
            pltpu.VMEM((count * rows, width // 2), jnp.float32),
            pltpu.VMEM((count * rows, width // 2), jnp.float32),
            pltpu.VMEM((len(cuts) * count * capacity, TPATCH), jnp.float32),
            pltpu.SMEM((len(cuts),), jnp.int32),
            pltpu.SemaphoreType.DMA,
            pltpu.SemaphoreType.DMA((rows // group,)),
            pltpu.SemaphoreType.DMA((len(sizes),)),
        ],
        compiler_params=params(),
        cost_estimate=pl.CostEstimate(flops=0, bytes_accessed=rows * tops * TPATCH * wide * 2, transcendentals=0),
        name="terms",
    )(offsets, increments, weights)
    given = []
    for cut in cuts:
        given.append(out[: len(cut) - 1])
        out = out[len(cut) - 1 :]
    return given


def sum_kernel(which, parity, patches, odd, places, *refs):
    slot_arrays, refs = refs[: len(which)], refs[len(which) :]
    wholes, outs, partial = [], refs[:-1], refs[-1]
    if parity is not None:
        wholes, outs = outs[:1], outs[1:]
    count = sum(out.shape[0] for out in outs) // patches
    capacity = slot_arrays[0].shape[0] // count
    totals = [partial.at[i] for i in range(len(slot_arrays))]
    for held in totals:
        held[...] = jnp.zeros_like(held)

    def one(k, carry):
        for row, slots, held in zip(which, slot_arrays, totals):
            at = pl.ds(places[row, k], count, stride=patches)
            held[at, :] = held[at, :] + slots[pl.ds(k, count, stride=capacity), :]
        return carry

    lax.fori_loop(0, capacity, one, 0, unroll=4)
    start = 0
    for out in outs:
        at = pl.ds(start, out.shape[0])
        total = totals[0][at, :]
        for more in totals[1:]:
            total = total + more[at, :]
        out[...] = total
        start += out.shape[0]
        if wholes:

            @pl.when(odd[0] == parity)
            def _():
                out[...] += wholes[0][at, :]


def patch_sums(odd, places, slot_arrays, which, patches, counts, whole=None, parity=None):
    wholes = [] if whole is None else [whole]
    return pl.pallas_call(
        functools.partial(sum_kernel, which, parity, patches),
        in_specs=in_smem(2) + in_vmem(len(wholes) + len(slot_arrays)),
        out_specs=in_vmem(len(counts)),
        out_shape=[jax.ShapeDtypeStruct((count * patches, TPATCH), jnp.float32) for count in counts],
        scratch_shapes=[pltpu.VMEM((len(slot_arrays), sum(counts) * patches, TPATCH), jnp.float32)],
        compiler_params=params(24 * 2**20),
        name="patch_sums",
    )(odd, places, *slot_arrays, *wholes)


def fields_kernel(first, settled, last, basis, thickness, wind_first, wind_second, *refs):
    depth, cov_first, cov_second, low_rows, high_rows, low_cols, high_cols = refs[-7:]
    rows, cols = depth.shape[1:]
    blocks = cols // TPATCH
    patches = rows * blocks
    lane = lax.broadcasted_iota(jnp.int32, (rows, TPATCH), 1)

    @pl.when(pl.program_id(0) == 0)
    def _():
        if first:
            low_cols[...] = refs[0][...]
            high_cols[...] = refs[1][...]
        else:
            low, high = (jnp.zeros((rows, TPATCH), jnp.float32) for _ in range(2))
            for f in range(FIELDS):
                lanes = TPATCH - (FIELDS - f) * HALO
                here = (lane >= lanes) & (lane < lanes + HALO)
                tile = refs[1][...] if f == FIELDS - 1 else refs[0][f]
                low = jnp.where(here, pltpu.roll(tile[:, :TPATCH], lanes, 1), low)
                high = jnp.where(here, pltpu.roll(tile[:, cols - TPATCH :], (lanes + HALO) % TPATCH, 1), high)
            low_cols[...] = low
            high_cols[...] = high

    for block in range(blocks):
        at = slice(block * TPATCH, (block + 1) * TPATCH)
        pieces = [slice(c * patches + block * rows, c * patches + (block + 1) * rows) for c in range(FIELDS)]
        east, north, thick = (settled[piece, :] + last[piece, :] for piece in pieces)
        values = (
            thickness[0, :, at] + thick,
            wind_first[0, :, at] + basis[0, :, at] * east + basis[1, :, at] * north,
            wind_second[0, :, at] + basis[2, :, at] * east + basis[3, :, at] * north,
        )
        for f, (ref, value) in enumerate(zip((depth, cov_first, cov_second), values)):
            ref[0, :, at] = value
            low_rows[f, :, at] = value[:HALO]
            high_rows[f, :, at] = value[rows - HALO :]
            lanes = ((first + pl.program_id(0)) * FIELDS + f) * HALO
            here = (lane >= lanes) & (lane < lanes + HALO)
            if block == 0:
                low_cols[...] = jnp.where(here, pltpu.roll(value, lanes, 1), low_cols[...])
            if block == blocks - 1:
                high_cols[...] = jnp.where(here, pltpu.roll(value, lanes + HALO, 1), high_cols[...])


def first_fields(place, levels, patches, settled, last, basis, thickness, wind_first, wind_second, metric, sides, fields, ends, later):
    first, begin, total, extra = place
    every, rows, cols = thickness.shape
    fixed = lambda shape: pl.BlockSpec(shape, lambda l: (0,) * len(shape))
    of_level = pl.BlockSpec((1, rows, cols), lambda l: (first + l, 0, 0))
    of_ends = pl.BlockSpec((FIELDS, HALO, cols), lambda l: (first - begin + l, 0, 0))
    of_patches = pl.BlockSpec((FIELDS * patches, TPATCH), lambda l: (l, 0))
    shapes = [(every, rows, cols)] * 3 + [(total * FIELDS + extra, HALO, cols)] * 2 + [(rows, TPATCH)] * 2
    beside = sides if ends else metric
    given = [*fields, *ends]
    aliases = {8 + i: i for i in range(len(fields))}
    aliases.update({8 + len(fields) + i: FIELDS + i for i in range(len(ends))})
    out = pl.pallas_call(
        functools.partial(fields_kernel, first - begin),
        grid=(levels,),
        in_specs=[of_patches, of_patches, fixed(basis.shape)]
        + [of_level] * 3
        + [fixed(array.shape) for array in beside]
        + in_hbm(len(given) + len(later)),
        out_specs=[of_level] * 3 + [of_ends] * 2 + [fixed((rows, TPATCH))] * 2,
        out_shape=[jax.ShapeDtypeStruct(shape, jnp.float32) for shape in shapes],
        input_output_aliases=aliases,
        compiler_params=params(32 * 2**20),
        name="first_fields",
    )(settled, last, basis, thickness, wind_first, wind_second, *beside, *given, *later)
    return out[:3], out[3:5], out[5:]


def entries_kernel(diag, cross, left, right, *refs):
    outs, i, count = refs[-2:], pl.program_id(0), pl.num_programs(0)
    rows, cols = cross.shape
    for out, at in zip(outs, (0, rows - HALO)):
        for f in range(FIELDS):

            @pl.when((i == f) & (i < count - 1))
            def _():
                out[0] = cross[at : at + HALO, :] if f == FIELDS - 1 else diag[f, at : at + HALO, :]

        @pl.when(i == count - 1)
        def _():
            out[...] = jnp.zeros_like(out)
            out[0, :, :TPATCH] = left[at : at + HALO, :]
            out[0, :, TPATCH : 2 * TPATCH] = right[at : at + HALO, :]


def last_entries(extra, ends, diag, cross, sides, later):
    whole, cols = ends[0].shape[0], ends[0].shape[-1]
    entry = pl.BlockSpec((1, HALO, cols), lambda i: (whole - extra + i, 0, 0))
    fixed = lambda array: pl.BlockSpec(array.shape, lambda i: (0,) * array.ndim)
    given = (diag, cross, *sides)
    return pl.pallas_call(
        entries_kernel,
        grid=(extra,),
        in_specs=[fixed(array) for array in given] + in_hbm(len(ends) + len(later)),
        out_specs=[entry] * 2,
        out_shape=[jax.ShapeDtypeStruct(end.shape, jnp.float32) for end in ends],
        input_output_aliases={len(given) + i: i for i in range(len(ends))},
        compiler_params=params(16 * 2**20),
        name="last_entries",
    )(*given, *ends, *later)


def rim_tile(lanes, left, right):
    lane = lax.broadcasted_iota(jnp.int32, left.shape, 1)
    return jnp.where(
        lane < HALO,
        pltpu.roll(right, (TPATCH - lanes) % TPATCH, 1),
        jnp.where(lane >= TPATCH - HALO, pltpu.roll(left, TPATCH - HALO - lanes, 1), 0.0),
    )


def upwind(face, behind, ahead):
    return face * jnp.where(face > 0.0, behind, ahead)


def steps_kernel(skipped, total_rows, spot, rotation, diag, cross, *refs):
    metric_halos, halos, parts = refs[:4], refs[4:8], refs[8 : 8 + FIELDS]
    outs, done, rimmed, wall = refs[-FIELDS - 3 : -3], refs[-3], refs[-2], refs[-1]
    done[...] = jnp.zeros_like(done)
    rows, cols = parts[0].shape[1:]
    ext_rows, ext_cols = rows + SUB, cols + TPATCH
    panel_rows = total_rows // PANELS
    l = skipped + pl.program_id(0)

    def columns(below, above, *sides):
        last = below.shape[0] - 1
        corners = lambda n: [end[last, :, n * TPATCH : (n + 1) * TPATCH] for end in (above, below)]
        return [jnp.concatenate([side[...]] + corners(n), axis=0) for n, side in enumerate(sides)]

    def with_rim(core, above, below, lanes, sides):
        return jnp.concatenate([jnp.concatenate([core, above, below], axis=0), rim_tile(lanes, *sides)], axis=1)

    @pl.when(pl.program_id(0) == 0)
    def _():
        below, above = metric_halos[:2]
        sides, entry = columns(*metric_halos), below.shape[0] - 1 - FIELDS
        for f in range(FIELDS):
            core = cross[...] if f == FIELDS - 1 else diag[f]
            lanes = TPATCH - (FIELDS - f) * HALO
            rimmed[f] = with_rim(core, above[entry + f], below[entry + f], lanes, sides) * (COURANT * 0.5)
        column = lax.broadcasted_iota(jnp.int32, wall.shape, 1)
        walled = ((spot[2] == 0) & (column == 0)) | ((spot[2] == spot[3] - 1) & (column == cols))
        wall[...] = jnp.where(walled, 0.0, 1.0)

    turns = []
    for edge in (0, rows):
        upper = lax.rem(spot[1] * rows + edge, total_rows)
        lower = lax.rem(upper + total_rows - 1, total_rows)
        joint = lax.rem(upper, panel_rows) == 0
        codes = [rotation[0, upper // panel_rows], rotation[1, lower // panel_rows]]
        turns.append([factor for code in codes for factor in quarter_turn(jnp.where(joint, code, 0))])

    sides = columns(*halos)
    depth, cov_first, cov_second = (
        with_rim(
            parts[f][0], halos[1][l * FIELDS + f], halos[0][l * FIELDS + f], (l * FIELDS + f) * HALO, sides
        )
        for f in range(FIELDS)
    )
    before = lambda v, axis: pltpu.roll(v, 1, axis)
    after = lambda v, axis: pltpu.roll(v, v.shape[axis] - 1, axis)
    piece = lambda v, start: v[start : start + SUB]
    joints = ((0, rows, 0), (rows, rows - SUB, 1)), ((rows - SUB, rows, 1), (rows, 0, 0))
    depth = depth * GRADIENT_HALF
    for _ in range(STEPS):
        con_first = rimmed[0] * cov_first + rimmed[2] * cov_second
        con_second = rimmed[2] * cov_first + rimmed[1] * cov_second
        depth_below, depth_above = before(depth, 0), after(depth, 0)
        second_below = before(con_second, 0)
        second_above = after(con_second, 0)
        row = lax.broadcasted_iota(jnp.int32, (SUB, ext_cols), 0)
        below, above = [], []
        for at, source, joint in joints[0]:
            turned = turns[joint][0] * piece(second_below, at) + turns[joint][1] * before(piece(con_first, source), 0)
            below.append(jnp.where(row == 0, turned, piece(second_below, at)))
        second_below = jnp.concatenate([below[0], second_below[SUB:rows], below[1]], axis=0)
        flux_below = upwind(con_second + second_below, depth_below, depth)
        for at, source, joint in joints[1]:
            turned = turns[joint][2] * piece(second_above, at) + turns[joint][3] * after(piece(con_first, source), 0)
            second = jnp.where(row == SUB - 1, turned, piece(second_above, at))
            above.append(upwind(piece(con_second, at) + second, piece(depth, at), piece(depth_above, at)))
        flux_above = jnp.concatenate([after(flux_below, 0)[: rows - SUB]] + above, axis=0)
        depth_left, depth_right = before(depth, 1), after(depth, 1)
        flux_left = upwind((con_first + before(con_first, 1)) * wall[0:1, :], depth_left, depth)
        flux_right = after(flux_left, 1)
        cov_first = cov_first - (depth_right - depth_left)
        cov_second = cov_second - (depth_above - depth_below)
        depth = depth - ((flux_right - flux_left) + (flux_above - flux_below))
    for ref, value in zip(outs, (depth * (1.0 / GRADIENT_HALF), cov_first, cov_second)):
        ref[0] = value[:rows, :cols]


def steps(first, count, skipped, total_rows, spot, rotation, diag, cross, metric_halos, halos, parts, so_far):
    levels, rows, cols = parts[0].shape
    assert total_rows // PANELS % rows == 0
    fixed = lambda array: pl.BlockSpec(array.shape, lambda l: (0,) * array.ndim)
    of_level = pl.BlockSpec((1, rows, cols), lambda l: (first + l, 0, 0))
    given = (diag, cross, *metric_halos, *halos)
    before = 2 + len(given) + len(parts)
    return pl.pallas_call(
        functools.partial(steps_kernel, skipped, total_rows),
        grid=(count,),
        in_specs=in_smem(2) + [fixed(array) for array in given] + [of_level] * FIELDS + in_hbm(len(so_far)),
        out_specs=[of_level] * FIELDS + [pl.BlockSpec((SUB, TPATCH), lambda l: (0, 0))],
        out_shape=[jax.ShapeDtypeStruct((levels, rows, cols), jnp.float32)] * FIELDS
        + [jax.ShapeDtypeStruct((SUB, TPATCH), jnp.float32)],
        input_output_aliases={before + i: i for i in range(len(so_far))},
        scratch_shapes=[
            pltpu.VMEM((FIELDS, rows + SUB, cols + TPATCH), jnp.float32),
            pltpu.VMEM((SUB, cols + TPATCH), jnp.float32),
        ],
        compiler_params=params(32 * 2**20),
        name="steps",
    )(spot, rotation, *given, *parts, *so_far)


def quarter_turn(code):
    cosine = (code == 0).astype(jnp.float32) - (code == 2).astype(jnp.float32)
    sine_value = (code == 1).astype(jnp.float32) - (code == 3).astype(jnp.float32)
    return (cosine, sine_value)


def shift(array, axis, by, closed):
    size = lax.axis_size(axis)
    pairs = [(i, (i + by) % size) for i in range(size) if closed or 0 <= i + by < size]
    return lax.ppermute(array, axis, pairs)


def together(*arrays):
    return lax.optimization_barrier(arrays)


def body(
    increments,
    remap_weights,
    dest_offset,
    slot_patch,
    rotation,
    basis,
    inv_metric_diag,
    inv_metric_cross,
    thickness,
    wind_first,
    wind_second,
):
    levels, rows, cols = thickness.shape
    tx_count, ty_count = lax.axis_size("tx"), lax.axis_size("ty")
    tx_index, ty_index = lax.axis_index("tx"), lax.axis_index("ty")
    owners, capacity = slot_patch.shape[2:]
    blocks = cols // TPATCH
    patches = rows * blocks
    bounds = [0]
    while bounds[-1] < levels:
        bounds.append(min(levels, bounds[-1] + CHUNKS[len(bounds) - 1]))
    parts = len(bounds) - 1

    evens, odds = range(0, ty_count, 2), range(1, ty_count, 2)
    swap = [(b, b + 1) for b in evens] + [(b, b - 1) for b in odds]
    send = lambda array, pairs: lax.ppermute(array, "ty", pairs)

    to_next = [(b, (b + 2) % ty_count) for b in range(ty_count)]
    places = slot_patch.reshape(owners, capacity)
    places = (places % blocks) * rows + places // blocks
    ahead = [shift(slot_patch.reshape(owners, capacity), "ty", -by, True) for by in (1, 2)]
    spot = jnp.stack([ty_index % 2, ty_index, tx_index, jnp.int32(tx_count)])

    offsets = dest_offset.transpose(0, 1, 3, 2).reshape(-1, dest_offset.shape[2])
    counts = [FIELDS * (last - first) for first, last in zip(bounds[:-1], bounds[1:])]
    wide = [bounds[pair[0]] for pair in PAIRS] + [levels]
    cuts = [bounds, wide] + [bounds] * (owners - 3) + [wide]
    own, first, second, far = terms(cuts, capacity, offsets, increments, remap_weights)
    *far, ahead[0], ahead[1] = together(*far, *ahead)
    places_next, places_second = ((p % blocks) * rows + p // blocks for p in ahead)
    thirds = [send(slots, to_next) for slots in far]
    metric = (inv_metric_diag, inv_metric_cross)
    token, results, finished = spot, [], []

    def steps_on(n, first, count, results):
        skipped = first - bounds[GROUPS[n][0]]
        return steps(first, count, skipped, rows * ty_count, spot, rotation, *metric, halos[0], halos[n], fields, results)

    across, last, settled, ends, sides, fields, halos = {}, {}, {}, {}, {}, [], []
    for step in ORDER:
        kind, n = step[0], int(step[1:])
        if kind == "P":
            chunks = PAIRS[n]
            paired = patch_sums(token, places_next, [thirds[n], first[n]], (3, 1), patches, [counts[j] for j in chunks])
            token, *paired = together(token, *paired)
            for j, part in zip(chunks, paired):
                across[j] = send(part, swap)
        elif kind == "J":
            (joined,) = patch_sums(token, places_second, [second[n]], (2,), patches, [counts[n]], across[n], 0)
            token, joined = together(token, joined)
            last[n] = send(joined, to_next)
        elif kind == "S":
            (settled[n],) = patch_sums(token, places, [own[n]], (0,), patches, [counts[n]], across[n], 1)
            token, settled[n] = together(token, settled[n])
        elif kind == "F":
            (g,) = (i for i, group in enumerate(GROUPS) if n in group)
            begin = bounds[GROUPS[g][0]]
            place = (bounds[n], begin, bounds[GROUPS[g][-1] + 1] - begin, 1 if g else 1 + FIELDS)
            token, ready = together(token, settled[n])
            fields, ends[g], sides[g] = first_fields(
                place, bounds[n + 1] - bounds[n], patches, ready, last[n], basis, thickness, wind_first, wind_second,
                metric, sides.get(g), fields, ends.get(g, []),
                halos[0] if g and n in LATE else [],
            )
            token, *sides[g] = together(token, *sides[g])
        else:
            low_cols, high_cols = sides[n]
            beside = [shift(high_cols, "tx", 1, False), shift(low_cols, "tx", -1, False)]

            if n == len(GROUPS) - 1:
                for first, count in EARLY:
                    *results, finished = steps_on(0, first, count, results)
                    finished = [finished]
            high_rows, low_rows = reversed(last_entries(1 if n else 1 + FIELDS, ends[n], *metric, beside, finished))
            halos.append([shift(high_rows, "ty", 1, True), shift(low_rows, "ty", -1, True), *beside])

    done = EARLY[-1][0] + EARLY[-1][1] if EARLY else 0
    for n, group in enumerate(GROUPS):
        first, end = max(done, bounds[group[0]]), bounds[group[-1] + 1]
        *results, _ = steps_on(n, first, end - first, results)
    return tuple(results)


def solution(mesh):
    in_specs = (
        P(None, None, "tx", "ty"),
        P("tx", "ty", None, None, None, None),
        P("tx", "ty", None, None),
        P("tx", "ty", None, None),
        P(),
        P(None, "ty", "tx"),
        P(None, "ty", "tx"),
        P("ty", "tx"),
        P(None, "ty", "tx"),
        P(None, "ty", "tx"),
        P(None, "ty", "tx"),
    )
    out_specs = (P(None, "ty", "tx"), P(None, "ty", "tx"), P(None, "ty", "tx"))
    return jax.shard_map(body, mesh=mesh, in_specs=in_specs, out_specs=out_specs, check_vma=False)
```

```python
import functools

import jax
import jax.numpy as jnp
from jax import lax
from jax.experimental import pallas as pl
from jax.experimental.pallas import tpu as pltpu
from jax.sharding import PartitionSpec as P

PANELS = 4
STEPS = 4
TPATCH = 128
HALO = 4
SUB = 8
FIELDS = 3
COURANT = 0.15
GRADIENT = 0.3
GRADIENT_HALF = GRADIENT * 0.5
CHUNKS = (2, 2, 2, 2)
PAIRS = ((0,), (1,), (2,), (3,))
GROUPS = ((0, 1), (2, 3))
AFTER = {0: (1,), 1: (2,)}
EARLY = ((0, 2),)
ORDER = (
    "P0", "P1", "P2", "J0", "P3", "J1", "S0", "S1", "J2", "F0", "J3", "S2", "S3", "F1", "F2", "H0", "F3", "H1",
)
GROUP = 16
VMEM = 48 * 2**20

ROWS_BY_ROWS = (((1,), (1,)), ((), ()))


def params(limit=VMEM):
    return pltpu.CompilerParams(vmem_limit_bytes=limit)


def in_vmem(count):
    return [pl.BlockSpec(memory_space=pltpu.VMEM)] * count


def in_smem(count):
    return [pl.BlockSpec(memory_space=pltpu.SMEM)] * count


def in_hbm(count):
    return [pl.BlockSpec(memory_space=pl.ANY)] * count


def spread(source, left, right):
    fields, levels, rows, width = source.shape
    half = width // 2
    for l in range(levels):
        for c in range(fields):
            at = pl.ds((l * fields + c) * rows, rows)
            left[at, :] = source[c, l, :, :half].astype(jnp.float32)
            right[at, :] = source[c, l, :, half:].astype(jnp.float32)


def row_block(left, right, s, count):
    at = pl.ds(s, count, stride=left.shape[0] // count)
    return jnp.concatenate([left[at, :], right[at, :]], axis=1).astype(jnp.bfloat16)


def write_out(cuts, fields, capacity, slots, outs, sems):
    count, copies = fields * cuts[0][-1], []
    starts = [(o * count + fields * first) * capacity for o, cut in enumerate(cuts) for first in cut[:-1]]
    for i, (start, out) in enumerate(zip(starts, outs)):
        copies.append(pltpu.make_async_copy(slots.at[pl.ds(start, out.shape[0])], out, sems.at[i]))
        copies[-1].start()
    for copy in copies:
        copy.wait()


def far_terms_kernel(bounds, owner, offsets, increments, weights, *refs):
    fields, levels, rows, _ = increments.shape
    count, tops = fields * levels, offsets.shape[0]
    parts = len(bounds) - 1
    outs, (held, source, left, right, order, source_sem, held_sem) = refs[:parts], refs[parts:]
    capacity = held.shape[0]
    first = pltpu.make_async_copy(increments, source, source_sem)
    first.start()

    def fetch(m, k):
        return pltpu.make_async_copy(weights.at[m], held.at[k], held_sem.at[k])

    def look(s, found):
        for t in range(tops):
            order[found] = s * tops + t
            found = found + (offsets[t, s] == owner).astype(jnp.int32)
        return found

    found = lax.fori_loop(0, rows, look, 0, unroll=8)

    @pl.loop(0, found)
    def _(k):
        fetch(order[k], k).start()

    first.wait()
    spread(source, left, right)
    group = max(g for g in range(1, GROUP + 1) if capacity % g == 0)

    @pl.loop(0, capacity // group)
    def _(g):
        for j in range(group):
            k = g * group + j

            @pl.when(k < found)
            def _():
                fetch(0, k).wait()

        for j in range(group):
            k = g * group + j
            s = order[jnp.minimum(k, found - 1)] // tops
            term = lax.dot_general(
                row_block(left, right, s, count), held[k], ROWS_BY_ROWS, preferred_element_type=jnp.float32
            )
            term = jnp.where(k < found, term, 0.0)
            for out, first, last in zip(outs, bounds[:-1], bounds[1:]):
                size = fields * (last - first)
                out[pl.ds(k, size, stride=capacity), :] = term[fields * first : fields * last]


def far_terms(bounds, owners, capacity, offsets, increments, weights):
    fields, levels, rows, width = increments.shape
    tops, wide = offsets.shape[0], weights.shape[-1]
    count, parts = fields * levels, len(bounds) - 1
    sizes = [fields * (last - first) * capacity for first, last in zip(bounds[:-1], bounds[1:])]
    return pl.pallas_call(
        functools.partial(far_terms_kernel, bounds, owners - 1),
        in_specs=in_smem(1) + in_hbm(2),
        out_specs=in_vmem(parts),
        out_shape=[jax.ShapeDtypeStruct((size, TPATCH), jnp.float32) for size in sizes],
        scratch_shapes=[
            pltpu.VMEM((capacity, TPATCH, wide), jnp.bfloat16),
            pltpu.VMEM(increments.shape, jnp.bfloat16),
            pltpu.VMEM((count * rows, width // 2), jnp.float32),
            pltpu.VMEM((count * rows, width // 2), jnp.float32),
            pltpu.SMEM((rows * tops + 1,), jnp.int32),
            pltpu.SemaphoreType.DMA,
            pltpu.SemaphoreType.DMA((capacity,)),
        ],
        compiler_params=params(62 * 2**20),
        name="far_terms",
    )(offsets, increments, weights.reshape(rows * tops, TPATCH, wide))


def terms_kernel(cuts, later, group, capacity, offsets, increments, weights, *refs):
    fields, levels, rows, _ = increments.shape
    count, tops = fields * levels, offsets.shape[0]
    outs = refs[later:-9]
    held, source, left, right, slots, used, source_sem, held_sem, out_sem = refs[-9:]
    groups = rows // group
    first = pltpu.make_async_copy(increments, source, source_sem)
    first.start()

    def fetch(g):
        piece = pl.ds(g * group, group)
        return pltpu.make_async_copy(weights.at[piece], held.at[piece], held_sem.at[g])

    @pl.loop(0, groups)
    def _(g):
        fetch(g).start()

    for o in range(len(cuts) + 1):
        used[o] = 0
    slots[...] = jnp.zeros_like(slots)
    first.wait()
    spread(source, left, right)

    @pl.loop(0, groups)
    def _(g):
        fetch(g).wait()
        for j in range(group):
            s = g * group + j
            block = row_block(left, right, s, count)
            term = lax.dot_general(block, held[s], ROWS_BY_ROWS, preferred_element_type=jnp.float32)
            for t in range(tops):
                o = offsets[t, s]
                k = used[o]
                used[o] = k + 1
                at = pl.ds(o * (count * capacity) + k, count, stride=capacity)
                slots[at, :] = term[:, t * TPATCH : (t + 1) * TPATCH]

    write_out(cuts, fields, capacity, slots, outs, out_sem)


def terms(cuts, capacity, offsets, increments, weights, later):
    fields, levels, rows, width = increments.shape
    tops, wide = offsets.shape[0], weights.shape[-1]
    count = fields * levels
    group = max(g for g in range(1, GROUP + 1) if rows % g == 0)
    sizes = [last - first for cut in cuts for first, last in zip(cut[:-1], cut[1:])]
    weights = weights.reshape(rows, tops * TPATCH, wide)
    out = pl.pallas_call(
        functools.partial(terms_kernel, cuts, len(later), group, capacity),
        in_specs=in_smem(1) + in_hbm(2 + len(later)),
        out_specs=in_hbm(len(sizes)),
        out_shape=[jax.ShapeDtypeStruct((fields * size * capacity, TPATCH), jnp.float32) for size in sizes],
        scratch_shapes=[
            pltpu.VMEM(weights.shape, jnp.bfloat16),
            pltpu.VMEM(increments.shape, jnp.bfloat16),
            pltpu.VMEM((count * rows, width // 2), jnp.float32),
            pltpu.VMEM((count * rows, width // 2), jnp.float32),
            pltpu.VMEM(((len(cuts) + 1) * count * capacity, TPATCH), jnp.float32),
            pltpu.SMEM((len(cuts) + 1,), jnp.int32),
            pltpu.SemaphoreType.DMA,
            pltpu.SemaphoreType.DMA((rows // group,)),
            pltpu.SemaphoreType.DMA((len(sizes),)),
        ],
        compiler_params=params(),
        cost_estimate=pl.CostEstimate(flops=0, bytes_accessed=rows * tops * TPATCH * wide * 2, transcendentals=0),
        name="terms",
    )(offsets, increments, weights, *later)
    given = []
    for cut in cuts:
        given.append(out[: len(cut) - 1])
        out = out[len(cut) - 1 :]
    return given


def sum_kernel(which, parity, patches, odd, places, *refs):
    slot_arrays, refs = refs[: len(which)], refs[len(which) :]
    wholes, outs, partial = [], refs[:-1], refs[-1]
    if parity is not None:
        wholes, outs = outs[:1], outs[1:]
    count = sum(out.shape[0] for out in outs) // patches
    capacity = slot_arrays[0].shape[0] // count
    totals = [partial.at[i] for i in range(len(slot_arrays))]
    for held in totals:
        held[...] = jnp.zeros_like(held)

    def one(k, carry):
        for row, slots, held in zip(which, slot_arrays, totals):
            at = pl.ds(places[row, k], count, stride=patches)
            held[at, :] = held[at, :] + slots[pl.ds(k, count, stride=capacity), :]
        return carry

    lax.fori_loop(0, capacity, one, 0, unroll=4)
    start = 0
    for out in outs:
        at = pl.ds(start, out.shape[0])
        total = totals[0][at, :]
        for more in totals[1:]:
            total = total + more[at, :]
        out[...] = total
        start += out.shape[0]
        if wholes:

            @pl.when(odd[0] == parity)
            def _():
                out[...] += wholes[0][at, :]


def patch_sums(odd, places, slot_arrays, which, patches, counts, whole=None, parity=None):
    wholes = [] if whole is None else [whole]
    return pl.pallas_call(
        functools.partial(sum_kernel, which, parity, patches),
        in_specs=in_smem(2) + in_vmem(len(wholes) + len(slot_arrays)),
        out_specs=in_vmem(len(counts)),
        out_shape=[jax.ShapeDtypeStruct((count * patches, TPATCH), jnp.float32) for count in counts],
        scratch_shapes=[pltpu.VMEM((len(slot_arrays), sum(counts) * patches, TPATCH), jnp.float32)],
        compiler_params=params(24 * 2**20),
        name="patch_sums",
    )(odd, places, *slot_arrays, *wholes)


def fields_kernel(first, settled, last, basis, thickness, wind_first, wind_second, *refs):
    depth, cov_first, cov_second, low_rows, high_rows, low_cols, high_cols = refs[-7:]
    rows, cols = depth.shape[1:]
    blocks = cols // TPATCH
    patches = rows * blocks
    lane = lax.broadcasted_iota(jnp.int32, (rows, TPATCH), 1)

    @pl.when(pl.program_id(0) == 0)
    def _():
        if first:
            low_cols[...] = refs[0][...]
            high_cols[...] = refs[1][...]
        else:
            low, high = (jnp.zeros((rows, TPATCH), jnp.float32) for _ in range(2))
            for f in range(FIELDS):
                lanes = TPATCH - (FIELDS - f) * HALO
                here = (lane >= lanes) & (lane < lanes + HALO)
                tile = refs[1][...] if f == FIELDS - 1 else refs[0][f]
                low = jnp.where(here, pltpu.roll(tile[:, :TPATCH], lanes, 1), low)
                high = jnp.where(here, pltpu.roll(tile[:, cols - TPATCH :], (lanes + HALO) % TPATCH, 1), high)
            low_cols[...] = low
            high_cols[...] = high

    for block in range(blocks):
        at = slice(block * TPATCH, (block + 1) * TPATCH)
        pieces = [slice(c * patches + block * rows, c * patches + (block + 1) * rows) for c in range(FIELDS)]
        east, north, thick = (settled[piece, :] + last[piece, :] for piece in pieces)
        values = (
            thickness[0, :, at] + thick,
            wind_first[0, :, at] + basis[0, :, at] * east + basis[1, :, at] * north,
            wind_second[0, :, at] + basis[2, :, at] * east + basis[3, :, at] * north,
        )
        for f, (ref, value) in enumerate(zip((depth, cov_first, cov_second), values)):
            ref[0, :, at] = value
            low_rows[f, :, at] = value[:HALO]
            high_rows[f, :, at] = value[rows - HALO :]
            lanes = ((first + pl.program_id(0)) * FIELDS + f) * HALO
            here = (lane >= lanes) & (lane < lanes + HALO)
            if block == 0:
                low_cols[...] = jnp.where(here, pltpu.roll(value, lanes, 1), low_cols[...])
            if block == blocks - 1:
                high_cols[...] = jnp.where(here, pltpu.roll(value, lanes + HALO, 1), high_cols[...])


def first_fields(place, levels, patches, settled, last, basis, thickness, wind_first, wind_second, metric, sides, fields, ends, later):
    first, begin, total, extra = place
    every, rows, cols = thickness.shape
    fixed = lambda shape: pl.BlockSpec(shape, lambda l: (0,) * len(shape))
    of_level = pl.BlockSpec((1, rows, cols), lambda l: (first + l, 0, 0))
    of_ends = pl.BlockSpec((FIELDS, HALO, cols), lambda l: (first - begin + l, 0, 0))
    of_patches = pl.BlockSpec((FIELDS * patches, TPATCH), lambda l: (l, 0))
    shapes = [(every, rows, cols)] * 3 + [(total * FIELDS + extra, HALO, cols)] * 2 + [(rows, TPATCH)] * 2
    beside = sides if ends else metric
    given = [*fields, *ends]
    aliases = {8 + i: i for i in range(len(fields))}
    aliases.update({8 + len(fields) + i: FIELDS + i for i in range(len(ends))})
    out = pl.pallas_call(
        functools.partial(fields_kernel, first - begin),
        grid=(levels,),
        in_specs=[of_patches, of_patches, fixed(basis.shape)]
        + [of_level] * 3
        + [fixed(array.shape) for array in beside]
        + in_hbm(len(given) + len(later)),
        out_specs=[of_level] * 3 + [of_ends] * 2 + [fixed((rows, TPATCH))] * 2,
        out_shape=[jax.ShapeDtypeStruct(shape, jnp.float32) for shape in shapes],
        input_output_aliases=aliases,
        compiler_params=params(32 * 2**20),
        name="first_fields",
    )(settled, last, basis, thickness, wind_first, wind_second, *beside, *given, *later)
    return out[:3], out[3:5], out[5:]


def entries_kernel(diag, cross, left, right, *refs):
    outs, i, count = refs[-2:], pl.program_id(0), pl.num_programs(0)
    rows, cols = cross.shape
    for out, at in zip(outs, (0, rows - HALO)):
        for f in range(FIELDS):

            @pl.when((i == f) & (i < count - 1))
            def _():
                out[0] = cross[at : at + HALO, :] if f == FIELDS - 1 else diag[f, at : at + HALO, :]

        @pl.when(i == count - 1)
        def _():
            out[...] = jnp.zeros_like(out)
            out[0, :, :TPATCH] = left[at : at + HALO, :]
            out[0, :, TPATCH : 2 * TPATCH] = right[at : at + HALO, :]


def last_entries(extra, ends, diag, cross, sides, later):
    whole, cols = ends[0].shape[0], ends[0].shape[-1]
    entry = pl.BlockSpec((1, HALO, cols), lambda i: (whole - extra + i, 0, 0))
    fixed = lambda array: pl.BlockSpec(array.shape, lambda i: (0,) * array.ndim)
    given = (diag, cross, *sides)
    return pl.pallas_call(
        entries_kernel,
        grid=(extra,),
        in_specs=[fixed(array) for array in given] + in_hbm(len(ends) + len(later)),
        out_specs=[entry] * 2,
        out_shape=[jax.ShapeDtypeStruct(end.shape, jnp.float32) for end in ends],
        input_output_aliases={len(given) + i: i for i in range(len(ends))},
        compiler_params=params(16 * 2**20),
        name="last_entries",
    )(*given, *ends, *later)


def rim_tile(lanes, left, right):
    lane = lax.broadcasted_iota(jnp.int32, left.shape, 1)
    return jnp.where(
        lane < HALO,
        pltpu.roll(right, (TPATCH - lanes) % TPATCH, 1),
        jnp.where(lane >= TPATCH - HALO, pltpu.roll(left, TPATCH - HALO - lanes, 1), 0.0),
    )


def upwind(face, behind, ahead):
    return face * jnp.where(face > 0.0, behind, ahead)


def steps_kernel(skipped, total_rows, spot, rotation, diag, cross, *refs):
    metric_halos, halos, parts = refs[:4], refs[4:8], refs[8 : 8 + FIELDS]
    outs, done, rimmed, wall = refs[-FIELDS - 3 : -3], refs[-3], refs[-2], refs[-1]
    done[...] = jnp.zeros_like(done)
    rows, cols = parts[0].shape[1:]
    ext_rows, ext_cols = rows + SUB, cols + TPATCH
    panel_rows = total_rows // PANELS
    l = skipped + pl.program_id(0)

    def columns(below, above, *sides):
        last = below.shape[0] - 1
        corners = lambda n: [end[last, :, n * TPATCH : (n + 1) * TPATCH] for end in (above, below)]
        return [jnp.concatenate([side[...]] + corners(n), axis=0) for n, side in enumerate(sides)]

    def with_rim(core, above, below, lanes, sides):
        return jnp.concatenate([jnp.concatenate([core, above, below], axis=0), rim_tile(lanes, *sides)], axis=1)

    @pl.when(pl.program_id(0) == 0)
    def _():
        below, above = metric_halos[:2]
        sides, entry = columns(*metric_halos), below.shape[0] - 1 - FIELDS
        for f in range(FIELDS):
            core = cross[...] if f == FIELDS - 1 else diag[f]
            lanes = TPATCH - (FIELDS - f) * HALO
            rimmed[f] = with_rim(core, above[entry + f], below[entry + f], lanes, sides) * (COURANT * 0.5)
        column = lax.broadcasted_iota(jnp.int32, wall.shape, 1)
        walled = ((spot[2] == 0) & (column == 0)) | ((spot[2] == spot[3] - 1) & (column == cols))
        wall[...] = jnp.where(walled, 0.0, 1.0)

    turns = []
    for edge in (0, rows):
        upper = lax.rem(spot[1] * rows + edge, total_rows)
        lower = lax.rem(upper + total_rows - 1, total_rows)
        joint = lax.rem(upper, panel_rows) == 0
        codes = [rotation[0, upper // panel_rows], rotation[1, lower // panel_rows]]
        turns.append([factor for code in codes for factor in quarter_turn(jnp.where(joint, code, 0))])

    sides = columns(*halos)
    depth, cov_first, cov_second = (
        with_rim(
            parts[f][0], halos[1][l * FIELDS + f], halos[0][l * FIELDS + f], (l * FIELDS + f) * HALO, sides
        )
        for f in range(FIELDS)
    )
    before = lambda v, axis: pltpu.roll(v, 1, axis)
    after = lambda v, axis: pltpu.roll(v, v.shape[axis] - 1, axis)
    piece = lambda v, start: v[start : start + SUB]
    joints = ((0, rows, 0), (rows, rows - SUB, 1)), ((rows - SUB, rows, 1), (rows, 0, 0))
    depth = depth * GRADIENT_HALF
    for _ in range(STEPS):
        con_first = rimmed[0] * cov_first + rimmed[2] * cov_second
        con_second = rimmed[2] * cov_first + rimmed[1] * cov_second
        depth_below, depth_above = before(depth, 0), after(depth, 0)
        second_below = before(con_second, 0)
        second_above = after(con_second, 0)
        row = lax.broadcasted_iota(jnp.int32, (SUB, ext_cols), 0)
        below, above = [], []
        for at, source, joint in joints[0]:
            turned = turns[joint][0] * piece(second_below, at) + turns[joint][1] * before(piece(con_first, source), 0)
            below.append(jnp.where(row == 0, turned, piece(second_below, at)))
        second_below = jnp.concatenate([below[0], second_below[SUB:rows], below[1]], axis=0)
        flux_below = upwind(con_second + second_below, depth_below, depth)
        for at, source, joint in joints[1]:
            turned = turns[joint][2] * piece(second_above, at) + turns[joint][3] * after(piece(con_first, source), 0)
            second = jnp.where(row == SUB - 1, turned, piece(second_above, at))
            above.append(upwind(piece(con_second, at) + second, piece(depth, at), piece(depth_above, at)))
        flux_above = jnp.concatenate([after(flux_below, 0)[: rows - SUB]] + above, axis=0)
        depth_left, depth_right = before(depth, 1), after(depth, 1)
        flux_left = upwind((con_first + before(con_first, 1)) * wall[0:1, :], depth_left, depth)
        flux_right = after(flux_left, 1)
        cov_first = cov_first - (depth_right - depth_left)
        cov_second = cov_second - (depth_above - depth_below)
        depth = depth - ((flux_right - flux_left) + (flux_above - flux_below))
    for ref, value in zip(outs, (depth * (1.0 / GRADIENT_HALF), cov_first, cov_second)):
        ref[0] = value[:rows, :cols]


def steps(first, count, skipped, total_rows, spot, rotation, diag, cross, metric_halos, halos, parts, so_far):
    levels, rows, cols = parts[0].shape
    assert total_rows // PANELS % rows == 0
    fixed = lambda array: pl.BlockSpec(array.shape, lambda l: (0,) * array.ndim)
    of_level = pl.BlockSpec((1, rows, cols), lambda l: (first + l, 0, 0))
    given = (diag, cross, *metric_halos, *halos)
    before = 2 + len(given) + len(parts)
    return pl.pallas_call(
        functools.partial(steps_kernel, skipped, total_rows),
        grid=(count,),
        in_specs=in_smem(2) + [fixed(array) for array in given] + [of_level] * FIELDS + in_hbm(len(so_far)),
        out_specs=[of_level] * FIELDS + [pl.BlockSpec((SUB, TPATCH), lambda l: (0, 0))],
        out_shape=[jax.ShapeDtypeStruct((levels, rows, cols), jnp.float32)] * FIELDS
        + [jax.ShapeDtypeStruct((SUB, TPATCH), jnp.float32)],
        input_output_aliases={before + i: i for i in range(len(so_far))},
        scratch_shapes=[
            pltpu.VMEM((FIELDS, rows + SUB, cols + TPATCH), jnp.float32),
            pltpu.VMEM((SUB, cols + TPATCH), jnp.float32),
        ],
        compiler_params=params(32 * 2**20),
        name="steps",
    )(spot, rotation, *given, *parts, *so_far)


def quarter_turn(code):
    cosine = (code == 0).astype(jnp.float32) - (code == 2).astype(jnp.float32)
    sine_value = (code == 1).astype(jnp.float32) - (code == 3).astype(jnp.float32)
    return (cosine, sine_value)


def shift(array, axis, by, closed):
    size = lax.axis_size(axis)
    pairs = [(i, (i + by) % size) for i in range(size) if closed or 0 <= i + by < size]
    return lax.ppermute(array, axis, pairs)


def together(*arrays):
    return lax.optimization_barrier(arrays)


def body(
    increments,
    remap_weights,
    dest_offset,
    slot_patch,
    rotation,
    basis,
    inv_metric_diag,
    inv_metric_cross,
    thickness,
    wind_first,
    wind_second,
):
    levels, rows, cols = thickness.shape
    tx_count, ty_count = lax.axis_size("tx"), lax.axis_size("ty")
    tx_index, ty_index = lax.axis_index("tx"), lax.axis_index("ty")
    owners, capacity = slot_patch.shape[2:]
    blocks = cols // TPATCH
    patches = rows * blocks
    bounds = [0]
    while bounds[-1] < levels:
        bounds.append(min(levels, bounds[-1] + CHUNKS[len(bounds) - 1]))
    parts = len(bounds) - 1

    evens, odds = range(0, ty_count, 2), range(1, ty_count, 2)
    swap = [(b, b + 1) for b in evens] + [(b, b - 1) for b in odds]
    send = lambda array, pairs: lax.ppermute(array, "ty", pairs)

    to_next = [(b, (b + 2) % ty_count) for b in range(ty_count)]
    places = slot_patch.reshape(owners, capacity)
    places = (places % blocks) * rows + places // blocks
    ahead = [shift(slot_patch.reshape(owners, capacity), "ty", -by, True) for by in (1, 2)]
    spot = jnp.stack([ty_index % 2, ty_index, tx_index, jnp.int32(tx_count)])

    offsets = dest_offset.transpose(0, 1, 3, 2).reshape(-1, dest_offset.shape[2])
    counts = [FIELDS * (last - first) for first, last in zip(bounds[:-1], bounds[1:])]
    wide = [bounds[pair[0]] for pair in PAIRS] + [levels]
    far = far_terms(bounds, owners, capacity, offsets, increments, remap_weights)
    cuts = [bounds, wide] + [bounds] * (owners - 3)
    own, first, second = terms(cuts, capacity, offsets, increments, remap_weights, [ahead[1]])
    *far, ahead[0], ahead[1] = together(*far, *ahead)
    places_next, places_second = ((p % blocks) * rows + p // blocks for p in ahead)
    thirds = [send(slots, to_next) for slots in far]
    metric = (inv_metric_diag, inv_metric_cross)
    token, results, finished = spot, [], []

    def steps_on(n, first, count, results):
        skipped = first - bounds[GROUPS[n][0]]
        return steps(first, count, skipped, rows * ty_count, spot, rotation, *metric, halos[0], halos[n], fields, results)

    across, last, settled, ends, sides, fields, halos = {}, {}, {}, {}, {}, [], []
    for step in ORDER:
        kind, n = step[0], int(step[1:])
        if kind == "P":
            chunks = PAIRS[n]
            paired = patch_sums(token, places_next, [thirds[n], first[n]], (3, 1), patches, [counts[j] for j in chunks])
            token, *paired = together(token, *paired)
            for j, part in zip(chunks, paired):
                across[j] = send(part, swap)
        elif kind == "J":
            (joined,) = patch_sums(token, places_second, [second[n]], (2,), patches, [counts[n]], across[n], 0)
            token, joined = together(token, joined)
            last[n] = send(joined, to_next)
        elif kind == "S":
            (settled[n],) = patch_sums(token, places, [own[n]], (0,), patches, [counts[n]], across[n], 1)
            token, settled[n] = together(token, settled[n])
        elif kind == "F":
            (g,) = (i for i, group in enumerate(GROUPS) if n in group)
            begin = bounds[GROUPS[g][0]]
            place = (bounds[n], begin, bounds[GROUPS[g][-1] + 1] - begin, 1 if g else 1 + FIELDS)
            token, ready = together(token, settled[n])
            fields, ends[g], sides[g] = first_fields(
                place, bounds[n + 1] - bounds[n], patches, ready, last[n], basis, thickness, wind_first, wind_second,
                metric, sides.get(g), fields, ends.get(g, []),
                [settled[j] for j in AFTER.get(n, ())],
            )
            token, *sides[g] = together(token, *sides[g])
        else:
            low_cols, high_cols = sides[n]
            beside = [shift(high_cols, "tx", 1, False), shift(low_cols, "tx", -1, False)]

            if n == len(GROUPS) - 1:
                for first, count in EARLY:
                    *results, finished = steps_on(0, first, count, results)
                    finished = [finished]
            waited = finished if n else [settled[parts - 1], *sides.get(1, [])[:1]]
            high_rows, low_rows = reversed(last_entries(1 if n else 1 + FIELDS, ends[n], *metric, beside, waited))
            halos.append([shift(high_rows, "ty", 1, True), shift(low_rows, "ty", -1, True), *beside])

    done = EARLY[-1][0] + EARLY[-1][1] if EARLY else 0
    for n, group in enumerate(GROUPS):
        first, end = max(done, bounds[group[0]]), bounds[group[-1] + 1]
        *results, _ = steps_on(n, first, end - first, results)
    return tuple(results)


def solution(mesh):
    in_specs = (
        P(None, None, "tx", "ty"),
        P("tx", "ty", None, None, None, None),
        P("tx", "ty", None, None),
        P("tx", "ty", None, None),
        P(),
        P(None, "ty", "tx"),
        P(None, "ty", "tx"),
        P("ty", "tx"),
        P(None, "ty", "tx"),
        P(None, "ty", "tx"),
        P(None, "ty", "tx"),
    )
    out_specs = (P(None, "ty", "tx"), P(None, "ty", "tx"), P(None, "ty", "tx"))
    return jax.shard_map(body, mesh=mesh, in_specs=in_specs, out_specs=out_specs, check_vma=False)
```

```python
import functools

import jax
import jax.numpy as jnp
from jax import lax
from jax.experimental import pallas as pl
from jax.experimental.pallas import tpu as pltpu
from jax.sharding import PartitionSpec as P

PANELS = 4
STEPS = 4
TPATCH = 128
HALO = 4
SUB = 8
FIELDS = 3
COURANT = 0.15
GRADIENT = 0.3
GRADIENT_HALF = GRADIENT * 0.5
CHUNKS = (2, 2, 2, 2)
PAIRS = ((0,), (1,), (2,), (3,))
GROUPS = ((0, 1), (2, 3))
AFTER = {0: (1,), 1: (2,)}
EARLY = ((0, 2),)
ORDER = (
    "P0", "P1", "P2", "J0", "P3", "J1", "S0", "S1", "J2", "F0", "J3", "S2", "S3", "F1", "F2", "H0", "F3", "H1",
)
GROUP = 16
VMEM = 48 * 2**20

ROWS_BY_ROWS = (((1,), (1,)), ((), ()))


def params(limit=VMEM):
    return pltpu.CompilerParams(vmem_limit_bytes=limit)


def in_vmem(count):
    return [pl.BlockSpec(memory_space=pltpu.VMEM)] * count


def in_smem(count):
    return [pl.BlockSpec(memory_space=pltpu.SMEM)] * count


def in_hbm(count):
    return [pl.BlockSpec(memory_space=pl.ANY)] * count


def spread(source, left, right):
    fields, levels, rows, width = source.shape
    half = width // 2
    for l in range(levels):
        for c in range(fields):
            at = pl.ds((l * fields + c) * rows, rows)
            left[at, :] = source[c, l, :, :half].astype(jnp.float32)
            right[at, :] = source[c, l, :, half:].astype(jnp.float32)


def row_block(left, right, s, count):
    at = pl.ds(s, count, stride=left.shape[0] // count)
    return jnp.concatenate([left[at, :], right[at, :]], axis=1).astype(jnp.bfloat16)


def write_out(cuts, fields, capacity, slots, outs, sems):
    count, copies = fields * cuts[0][-1], []
    starts = [(o * count + fields * first) * capacity for o, cut in enumerate(cuts) for first in cut[:-1]]
    for i, (start, out) in enumerate(zip(starts, outs)):
        copies.append(pltpu.make_async_copy(slots.at[pl.ds(start, out.shape[0])], out, sems.at[i]))
        copies[-1].start()
    for copy in copies:
        copy.wait()


def far_terms_kernel(bounds, owner, offsets, increments, weights, *refs):
    fields, levels, rows, _ = increments.shape
    count, tops = fields * levels, offsets.shape[0]
    parts = len(bounds) - 1
    outs, (held, source, left, right, order, source_sem, held_sem) = refs[:parts], refs[parts:]
    capacity = held.shape[0]
    first = pltpu.make_async_copy(increments, source, source_sem)
    first.start()

    def fetch(m, k):
        return pltpu.make_async_copy(weights.at[m], held.at[k], held_sem.at[k])

    def look(s, found):
        for t in range(tops):
            order[found] = s * tops + t
            found = found + (offsets[t, s] == owner).astype(jnp.int32)
        return found

    found = lax.fori_loop(0, rows, look, 0, unroll=8)

    @pl.loop(0, found)
    def _(k):
        fetch(order[k], k).start()

    first.wait()
    spread(source, left, right)
    group = max(g for g in range(1, GROUP + 1) if capacity % g == 0)

    @pl.loop(0, capacity // group)
    def _(g):
        for j in range(group):
            k = g * group + j

            @pl.when(k < found)
            def _():
                fetch(0, k).wait()

        for j in range(group):
            k = g * group + j
            s = order[jnp.minimum(k, found - 1)] // tops
            term = lax.dot_general(
                row_block(left, right, s, count), held[k], ROWS_BY_ROWS, preferred_element_type=jnp.float32
            )
            term = jnp.where(k < found, term, 0.0)
            for out, first, last in zip(outs, bounds[:-1], bounds[1:]):
                size = fields * (last - first)
                out[pl.ds(k, size, stride=capacity), :] = term[fields * first : fields * last]


def far_terms(bounds, owners, capacity, offsets, increments, weights):
    fields, levels, rows, width = increments.shape
    tops, wide = offsets.shape[0], weights.shape[-1]
    count, parts = fields * levels, len(bounds) - 1
    sizes = [fields * (last - first) * capacity for first, last in zip(bounds[:-1], bounds[1:])]
    return pl.pallas_call(
        functools.partial(far_terms_kernel, bounds, owners - 1),
        in_specs=in_smem(1) + in_hbm(2),
        out_specs=in_vmem(parts),
        out_shape=[jax.ShapeDtypeStruct((size, TPATCH), jnp.float32) for size in sizes],
        scratch_shapes=[
            pltpu.VMEM((capacity, TPATCH, wide), jnp.bfloat16),
            pltpu.VMEM(increments.shape, jnp.bfloat16),
            pltpu.VMEM((count * rows, width // 2), jnp.float32),
            pltpu.VMEM((count * rows, width // 2), jnp.float32),
            pltpu.SMEM((rows * tops + 1,), jnp.int32),
            pltpu.SemaphoreType.DMA,
            pltpu.SemaphoreType.DMA((capacity,)),
        ],
        compiler_params=params(62 * 2**20),
        name="far_terms",
    )(offsets, increments, weights.reshape(rows * tops, TPATCH, wide))


def terms_kernel(cuts, later, group, capacity, offsets, increments, weights, *refs):
    fields, levels, rows, _ = increments.shape
    count, tops = fields * levels, offsets.shape[0]
    outs = refs[later:-9]
    held, source, left, right, slots, used, source_sem, held_sem, out_sem = refs[-9:]
    groups = rows // group
    first = pltpu.make_async_copy(increments, source, source_sem)
    first.start()

    def fetch(g):
        piece = pl.ds(g * group, group)
        return pltpu.make_async_copy(weights.at[piece], held.at[piece], held_sem.at[g])

    @pl.loop(0, groups)
    def _(g):
        fetch(g).start()

    for o in range(len(cuts) + 1):
        used[o] = 0
    slots[...] = jnp.zeros_like(slots)
    first.wait()
    spread(source, left, right)

    @pl.loop(0, groups)
    def _(g):
        fetch(g).wait()
        for j in range(group):
            s = g * group + j
            block = row_block(left, right, s, count)
            term = lax.dot_general(block, held[s], ROWS_BY_ROWS, preferred_element_type=jnp.float32)
            for t in range(tops):
                o = offsets[t, s]
                k = used[o]
                used[o] = k + 1
                at = pl.ds(o * (count * capacity) + k, count, stride=capacity)
                slots[at, :] = term[:, t * TPATCH : (t + 1) * TPATCH]

    write_out(cuts, fields, capacity, slots, outs, out_sem)


def terms(cuts, capacity, offsets, increments, weights, later):
    fields, levels, rows, width = increments.shape
    tops, wide = offsets.shape[0], weights.shape[-1]
    count = fields * levels
    group = max(g for g in range(1, GROUP + 1) if rows % g == 0)
    sizes = [last - first for cut in cuts for first, last in zip(cut[:-1], cut[1:])]
    weights = weights.reshape(rows, tops * TPATCH, wide)
    out = pl.pallas_call(
        functools.partial(terms_kernel, cuts, len(later), group, capacity),
        in_specs=in_smem(1) + in_hbm(2 + len(later)),
        out_specs=in_hbm(len(sizes)),
        out_shape=[jax.ShapeDtypeStruct((fields * size * capacity, TPATCH), jnp.float32) for size in sizes],
        scratch_shapes=[
            pltpu.VMEM(weights.shape, jnp.bfloat16),
            pltpu.VMEM(increments.shape, jnp.bfloat16),
            pltpu.VMEM((count * rows, width // 2), jnp.float32),
            pltpu.VMEM((count * rows, width // 2), jnp.float32),
            pltpu.VMEM(((len(cuts) + 1) * count * capacity, TPATCH), jnp.float32),
            pltpu.SMEM((len(cuts) + 1,), jnp.int32),
            pltpu.SemaphoreType.DMA,
            pltpu.SemaphoreType.DMA((rows // group,)),
            pltpu.SemaphoreType.DMA((len(sizes),)),
        ],
        compiler_params=params(),
        cost_estimate=pl.CostEstimate(flops=0, bytes_accessed=rows * tops * TPATCH * wide * 2, transcendentals=0),
        name="terms",
    )(offsets, increments, weights, *later)
    given = []
    for cut in cuts:
        given.append(out[: len(cut) - 1])
        out = out[len(cut) - 1 :]
    return given


def sum_kernel(which, parity, patches, odd, places, *refs):
    slot_arrays, refs = refs[: len(which)], refs[len(which) :]
    wholes, outs, partial = [], refs[:-1], refs[-1]
    if parity is not None:
        wholes, outs = outs[:1], outs[1:]
    count = sum(out.shape[0] for out in outs) // patches
    capacity = slot_arrays[0].shape[0] // count
    totals = [partial.at[i] for i in range(len(slot_arrays))]
    for held in totals:
        held[...] = jnp.zeros_like(held)

    def one(k, carry):
        for row, slots, held in zip(which, slot_arrays, totals):
            at = pl.ds(places[row, k], count, stride=patches)
            held[at, :] = held[at, :] + slots[pl.ds(k, count, stride=capacity), :]
        return carry

    lax.fori_loop(0, capacity, one, 0, unroll=4)
    start = 0
    for out in outs:
        at = pl.ds(start, out.shape[0])
        total = totals[0][at, :]
        for more in totals[1:]:
            total = total + more[at, :]
        out[...] = total
        start += out.shape[0]
        if wholes:

            @pl.when(odd[0] == parity)
            def _():
                out[...] += wholes[0][at, :]


def patch_sums(odd, places, slot_arrays, which, patches, counts, whole=None, parity=None):
    wholes = [] if whole is None else [whole]
    return pl.pallas_call(
        functools.partial(sum_kernel, which, parity, patches),
        in_specs=in_smem(2) + in_vmem(len(wholes) + len(slot_arrays)),
        out_specs=in_vmem(len(counts)),
        out_shape=[jax.ShapeDtypeStruct((count * patches, TPATCH), jnp.float32) for count in counts],
        scratch_shapes=[pltpu.VMEM((len(slot_arrays), sum(counts) * patches, TPATCH), jnp.float32)],
        compiler_params=params(24 * 2**20),
        name="patch_sums",
    )(odd, places, *slot_arrays, *wholes)


def fields_kernel(first, settled, last, basis, thickness, wind_first, wind_second, *refs):
    depth, cov_first, cov_second, low_rows, high_rows, low_cols, high_cols = refs[-7:]
    rows, cols = depth.shape[1:]
    blocks = cols // TPATCH
    patches = rows * blocks
    lane = lax.broadcasted_iota(jnp.int32, (rows, TPATCH), 1)

    @pl.when(pl.program_id(0) == 0)
    def _():
        if first:
            low_cols[...] = refs[0][...]
            high_cols[...] = refs[1][...]
        else:
            low, high = (jnp.zeros((rows, TPATCH), jnp.float32) for _ in range(2))
            for f in range(FIELDS):
                lanes = TPATCH - (FIELDS - f) * HALO
                here = (lane >= lanes) & (lane < lanes + HALO)
                tile = refs[1][...] if f == FIELDS - 1 else refs[0][f]
                low = jnp.where(here, pltpu.roll(tile[:, :TPATCH], lanes, 1), low)
                high = jnp.where(here, pltpu.roll(tile[:, cols - TPATCH :], (lanes + HALO) % TPATCH, 1), high)
            low_cols[...] = low
            high_cols[...] = high

    for block in range(blocks):
        at = slice(block * TPATCH, (block + 1) * TPATCH)
        pieces = [slice(c * patches + block * rows, c * patches + (block + 1) * rows) for c in range(FIELDS)]
        east, north, thick = (settled[piece, :] + last[piece, :] for piece in pieces)
        values = (
            thickness[0, :, at] + thick,
            wind_first[0, :, at] + basis[0, :, at] * east + basis[1, :, at] * north,
            wind_second[0, :, at] + basis[2, :, at] * east + basis[3, :, at] * north,
        )
        for f, (ref, value) in enumerate(zip((depth, cov_first, cov_second), values)):
            ref[0, :, at] = value
            low_rows[f, :, at] = value[:HALO]
            high_rows[f, :, at] = value[rows - HALO :]
            lanes = ((first + pl.program_id(0)) * FIELDS + f) * HALO
            here = (lane >= lanes) & (lane < lanes + HALO)
            if block == 0:
                low_cols[...] = jnp.where(here, pltpu.roll(value, lanes, 1), low_cols[...])
            if block == blocks - 1:
                high_cols[...] = jnp.where(here, pltpu.roll(value, lanes + HALO, 1), high_cols[...])


def first_fields(place, levels, patches, settled, last, basis, thickness, wind_first, wind_second, metric, sides, fields, ends, later):
    first, begin, total, extra = place
    every, rows, cols = thickness.shape
    fixed = lambda shape: pl.BlockSpec(shape, lambda l: (0,) * len(shape))
    of_level = pl.BlockSpec((1, rows, cols), lambda l: (first + l, 0, 0))
    of_ends = pl.BlockSpec((FIELDS, HALO, cols), lambda l: (first - begin + l, 0, 0))
    of_patches = pl.BlockSpec((FIELDS * patches, TPATCH), lambda l: (l, 0))
    shapes = [(every, rows, cols)] * 3 + [(total * FIELDS + extra, HALO, cols)] * 2 + [(rows, TPATCH)] * 2
    beside = sides if ends else metric
    given = [*fields, *ends]
    aliases = {8 + i: i for i in range(len(fields))}
    aliases.update({8 + len(fields) + i: FIELDS + i for i in range(len(ends))})
    out = pl.pallas_call(
        functools.partial(fields_kernel, first - begin),
        grid=(levels,),
        in_specs=[of_patches, of_patches, fixed(basis.shape)]
        + [of_level] * 3
        + [fixed(array.shape) for array in beside]
        + in_hbm(len(given) + len(later)),
        out_specs=[of_level] * 3 + [of_ends] * 2 + [fixed((rows, TPATCH))] * 2,
        out_shape=[jax.ShapeDtypeStruct(shape, jnp.float32) for shape in shapes],
        input_output_aliases=aliases,
        compiler_params=params(32 * 2**20),
        name="first_fields",
    )(settled, last, basis, thickness, wind_first, wind_second, *beside, *given, *later)
    return out[:3], out[3:5], out[5:]


def entries_kernel(diag, cross, left, right, *refs):
    outs, i, count = refs[-2:], pl.program_id(0), pl.num_programs(0)
    rows, cols = cross.shape
    for out, at in zip(outs, (0, rows - HALO)):
        for f in range(FIELDS):

            @pl.when((i == f) & (i < count - 1))
            def _():
                out[0] = cross[at : at + HALO, :] if f == FIELDS - 1 else diag[f, at : at + HALO, :]

        @pl.when(i == count - 1)
        def _():
            out[...] = jnp.zeros_like(out)
            out[0, :, :TPATCH] = left[at : at + HALO, :]
            out[0, :, TPATCH : 2 * TPATCH] = right[at : at + HALO, :]


def last_entries(extra, ends, diag, cross, sides, later):
    whole, cols = ends[0].shape[0], ends[0].shape[-1]
    entry = pl.BlockSpec((1, HALO, cols), lambda i: (whole - extra + i, 0, 0))
    fixed = lambda array: pl.BlockSpec(array.shape, lambda i: (0,) * array.ndim)
    given = (diag, cross, *sides)
    return pl.pallas_call(
        entries_kernel,
        grid=(extra,),
        in_specs=[fixed(array) for array in given] + in_hbm(len(ends) + len(later)),
        out_specs=[entry] * 2,
        out_shape=[jax.ShapeDtypeStruct(end.shape, jnp.float32) for end in ends],
        input_output_aliases={len(given) + i: i for i in range(len(ends))},
        compiler_params=params(16 * 2**20),
        name="last_entries",
    )(*given, *ends, *later)


def rim_tile(lanes, left, right):
    lane = lax.broadcasted_iota(jnp.int32, left.shape, 1)
    return jnp.where(
        lane < HALO,
        pltpu.roll(right, (TPATCH - lanes) % TPATCH, 1),
        jnp.where(lane >= TPATCH - HALO, pltpu.roll(left, TPATCH - HALO - lanes, 1), 0.0),
    )


def upwind(face, behind, ahead):
    return face * jnp.where(face > 0.0, behind, ahead)


def steps_kernel(skipped, total_rows, given, *refs):
    if given == 2:
        spot, rotation, *refs = refs
    metric, refs = refs[:given], refs[given:]
    halos, parts = refs[:4], refs[4 : 4 + FIELDS]
    if given == 2:
        outs, (rimmed, factors, wall) = refs[-FIELDS - 3 : -3], refs[-3:]
    else:
        outs, (rimmed, factors, wall) = refs[-FIELDS:], metric
    rows, cols = parts[0].shape[1:]
    ext_rows, ext_cols = rows + SUB, cols + TPATCH
    panel_rows = total_rows // PANELS
    l = skipped + pl.program_id(0)

    def columns(below, above, *sides):
        last = below.shape[0] - 1
        corners = lambda n: [end[last, :, n * TPATCH : (n + 1) * TPATCH] for end in (above, below)]
        return [jnp.concatenate([side[...]] + corners(n), axis=0) for n, side in enumerate(sides)]

    def with_rim(core, above, below, lanes, sides):
        return jnp.concatenate([jnp.concatenate([core, above, below], axis=0), rim_tile(lanes, *sides)], axis=1)

    @pl.when(pl.program_id(0) == 0)
    def _():
        if given == 2:
            diag, cross = metric
            below, above = halos[:2]
            sides, entry = columns(*halos), below.shape[0] - 1 - FIELDS
            for f in range(FIELDS):
                core = cross[...] if f == FIELDS - 1 else diag[f]
                lanes = TPATCH - (FIELDS - f) * HALO
                rimmed[f] = with_rim(core, above[entry + f], below[entry + f], lanes, sides) * (COURANT * 0.5)
            column = lax.broadcasted_iota(jnp.int32, wall.shape, 1)
            walled = ((spot[2] == 0) & (column == 0)) | ((spot[2] == spot[3] - 1) & (column == cols))
            wall[...] = jnp.where(walled, 0.0, 1.0)
            row = lax.broadcasted_iota(jnp.int32, factors.shape, 0)
            value, n = jnp.zeros(factors.shape, jnp.float32), 0
            for edge in (0, rows):
                upper = lax.rem(spot[1] * rows + edge, total_rows)
                lower = lax.rem(upper + total_rows - 1, total_rows)
                joint = lax.rem(upper, panel_rows) == 0
                for code in (rotation[0, upper // panel_rows], rotation[1, lower // panel_rows]):
                    for factor in quarter_turn(jnp.where(joint, code, 0)):
                        value, n = jnp.where(row == n, factor, value), n + 1
            factors[...] = value

    wide = lambda n: jnp.concatenate([factors[n : n + 1, :]] * (ext_cols // TPATCH), axis=1)
    turns = [[wide(4 * joint + n) for n in range(4)] for joint in range(2)]
    sides = columns(*halos)
    depth, cov_first, cov_second = (
        with_rim(
            parts[f][0], halos[1][l * FIELDS + f], halos[0][l * FIELDS + f], (l * FIELDS + f) * HALO, sides
        )
        for f in range(FIELDS)
    )
    before = lambda v, axis: pltpu.roll(v, 1, axis)
    after = lambda v, axis: pltpu.roll(v, v.shape[axis] - 1, axis)
    piece = lambda v, start: v[start : start + SUB]
    joints = ((0, rows, 0), (rows, rows - SUB, 1)), ((rows - SUB, rows, 1), (rows, 0, 0))
    depth = depth * GRADIENT_HALF
    for _ in range(STEPS):
        con_first = rimmed[0] * cov_first + rimmed[2] * cov_second
        con_second = rimmed[2] * cov_first + rimmed[1] * cov_second
        depth_below, depth_above = before(depth, 0), after(depth, 0)
        second_below = before(con_second, 0)
        second_above = after(con_second, 0)
        row = lax.broadcasted_iota(jnp.int32, (SUB, ext_cols), 0)
        below, above = [], []
        for at, source, joint in joints[0]:
            turned = turns[joint][0] * piece(second_below, at) + turns[joint][1] * before(piece(con_first, source), 0)
            below.append(jnp.where(row == 0, turned, piece(second_below, at)))
        second_below = jnp.concatenate([below[0], second_below[SUB:rows], below[1]], axis=0)
        flux_below = upwind(con_second + second_below, depth_below, depth)
        for at, source, joint in joints[1]:
            turned = turns[joint][2] * piece(second_above, at) + turns[joint][3] * after(piece(con_first, source), 0)
            second = jnp.where(row == SUB - 1, turned, piece(second_above, at))
            above.append(upwind(piece(con_second, at) + second, piece(depth, at), piece(depth_above, at)))
        flux_above = jnp.concatenate([after(flux_below, 0)[: rows - SUB]] + above, axis=0)
        depth_left, depth_right = before(depth, 1), after(depth, 1)
        flux_left = upwind((con_first + before(con_first, 1)) * wall[0:1, :], depth_left, depth)
        flux_right = after(flux_left, 1)
        cov_first = cov_first - (depth_right - depth_left)
        cov_second = cov_second - (depth_above - depth_below)
        depth = depth - ((flux_right - flux_left) + (flux_above - flux_below))
    for ref, value in zip(outs, (depth * (1.0 / GRADIENT_HALF), cov_first, cov_second)):
        ref[0] = value[:rows, :cols]


def steps(first, count, skipped, total_rows, spot, rotation, metric, halos, parts, so_far):
    levels, rows, cols = parts[0].shape
    assert total_rows // PANELS % rows == 0
    fixed = lambda shape: pl.BlockSpec(shape, lambda l: (0,) * len(shape))
    of_level = pl.BlockSpec((1, rows, cols), lambda l: (first + l, 0, 0))
    given = (*metric, *halos)
    before = (2 if len(metric) == 2 else 0) + len(given) + len(parts)
    new = len(metric) == 2
    kept = [(FIELDS, rows + SUB, cols + TPATCH), (SUB, TPATCH), (SUB, cols + TPATCH)] if new else []
    return pl.pallas_call(
        functools.partial(steps_kernel, skipped, total_rows, len(metric)),
        grid=(count,),
        in_specs=in_smem(2 if new else 0)
        + [fixed(array.shape) for array in given]
        + [of_level] * FIELDS
        + in_hbm(len(so_far)),
        out_specs=[of_level] * FIELDS + [fixed(shape) for shape in kept],
        out_shape=[jax.ShapeDtypeStruct(shape, jnp.float32) for shape in [(levels, rows, cols)] * FIELDS + kept],
        input_output_aliases={before + i: i for i in range(len(so_far))},
        compiler_params=params(32 * 2**20),
        name="steps",
    )(*((spot, rotation) if new else ()), *given, *parts, *so_far)


def quarter_turn(code):
    cosine = (code == 0).astype(jnp.float32) - (code == 2).astype(jnp.float32)
    sine_value = (code == 1).astype(jnp.float32) - (code == 3).astype(jnp.float32)
    return (cosine, sine_value)


def shift(array, axis, by, closed):
    size = lax.axis_size(axis)
    pairs = [(i, (i + by) % size) for i in range(size) if closed or 0 <= i + by < size]
    return lax.ppermute(array, axis, pairs)


def together(*arrays):
    return lax.optimization_barrier(arrays)


def body(
    increments,
    remap_weights,
    dest_offset,
    slot_patch,
    rotation,
    basis,
    inv_metric_diag,
    inv_metric_cross,
    thickness,
    wind_first,
    wind_second,
):
    levels, rows, cols = thickness.shape
    tx_count, ty_count = lax.axis_size("tx"), lax.axis_size("ty")
    tx_index, ty_index = lax.axis_index("tx"), lax.axis_index("ty")
    owners, capacity = slot_patch.shape[2:]
    blocks = cols // TPATCH
    patches = rows * blocks
    bounds = [0]
    while bounds[-1] < levels:
        bounds.append(min(levels, bounds[-1] + CHUNKS[len(bounds) - 1]))
    parts = len(bounds) - 1

    evens, odds = range(0, ty_count, 2), range(1, ty_count, 2)
    swap = [(b, b + 1) for b in evens] + [(b, b - 1) for b in odds]
    send = lambda array, pairs: lax.ppermute(array, "ty", pairs)

    to_next = [(b, (b + 2) % ty_count) for b in range(ty_count)]
    places = slot_patch.reshape(owners, capacity)
    places = (places % blocks) * rows + places // blocks
    ahead = [shift(slot_patch.reshape(owners, capacity), "ty", -by, True) for by in (1, 2)]
    spot = jnp.stack([ty_index % 2, ty_index, tx_index, jnp.int32(tx_count)])

    offsets = dest_offset.transpose(0, 1, 3, 2).reshape(-1, dest_offset.shape[2])
    counts = [FIELDS * (last - first) for first, last in zip(bounds[:-1], bounds[1:])]
    wide = [bounds[pair[0]] for pair in PAIRS] + [levels]
    far = far_terms(bounds, owners, capacity, offsets, increments, remap_weights)
    cuts = [bounds, wide] + [bounds] * (owners - 3)
    own, first, second = terms(cuts, capacity, offsets, increments, remap_weights, [ahead[1]])
    *far, ahead[0], ahead[1] = together(*far, *ahead)
    places_next, places_second = ((p % blocks) * rows + p // blocks for p in ahead)
    thirds = [send(slots, to_next) for slots in far]
    metric = (inv_metric_diag, inv_metric_cross)
    token, results, finished = spot, [], []

    def steps_on(n, first, count, results, rimmed):
        skipped = first - bounds[GROUPS[n][0]]
        out = steps(
            first, count, skipped, rows * ty_count, spot, rotation, rimmed or metric, halos[n], fields, results
        )
        return out[:FIELDS], rimmed or out[FIELDS:]

    across, last, settled, ends, sides, fields, halos = {}, {}, {}, {}, {}, [], []
    for step in ORDER:
        kind, n = step[0], int(step[1:])
        if kind == "P":
            chunks = PAIRS[n]
            paired = patch_sums(token, places_next, [thirds[n], first[n]], (3, 1), patches, [counts[j] for j in chunks])
            token, *paired = together(token, *paired)
            for j, part in zip(chunks, paired):
                across[j] = send(part, swap)
        elif kind == "J":
            (joined,) = patch_sums(token, places_second, [second[n]], (2,), patches, [counts[n]], across[n], 0)
            token, joined = together(token, joined)
            last[n] = send(joined, to_next)
        elif kind == "S":
            (settled[n],) = patch_sums(token, places, [own[n]], (0,), patches, [counts[n]], across[n], 1)
            token, settled[n] = together(token, settled[n])
        elif kind == "F":
            (g,) = (i for i, group in enumerate(GROUPS) if n in group)
            begin = bounds[GROUPS[g][0]]
            place = (bounds[n], begin, bounds[GROUPS[g][-1] + 1] - begin, 1 if g else 1 + FIELDS)
            token, ready = together(token, settled[n])
            fields, ends[g], sides[g] = first_fields(
                place, bounds[n + 1] - bounds[n], patches, ready, last[n], basis, thickness, wind_first, wind_second,
                metric, sides.get(g), fields, ends.get(g, []),
                [settled[j] for j in AFTER.get(n, ())],
            )
            token, *sides[g] = together(token, *sides[g])
        else:
            low_cols, high_cols = sides[n]
            beside = [shift(high_cols, "tx", 1, False), shift(low_cols, "tx", -1, False)]

            if n == len(GROUPS) - 1:
                for first, count in EARLY:
                    results, finished = steps_on(0, first, count, results, finished)
            waited = finished if n else [settled[parts - 1], *sides.get(1, [])[:1]]
            high_rows, low_rows = reversed(last_entries(1 if n else 1 + FIELDS, ends[n], *metric, beside, waited[:1] if n else waited))
            halos.append([shift(high_rows, "ty", 1, True), shift(low_rows, "ty", -1, True), *beside])

    done = EARLY[-1][0] + EARLY[-1][1] if EARLY else 0
    for n, group in enumerate(GROUPS):
        first, end = max(done, bounds[group[0]]), bounds[group[-1] + 1]
        results, finished = steps_on(n, first, end - first, results, finished)
    return tuple(results)


def solution(mesh):
    in_specs = (
        P(None, None, "tx", "ty"),
        P("tx", "ty", None, None, None, None),
        P("tx", "ty", None, None),
        P("tx", "ty", None, None),
        P(),
        P(None, "ty", "tx"),
        P(None, "ty", "tx"),
        P("ty", "tx"),
        P(None, "ty", "tx"),
        P(None, "ty", "tx"),
        P(None, "ty", "tx"),
    )
    out_specs = (P(None, "ty", "tx"), P(None, "ty", "tx"), P(None, "ty", "tx"))
    return jax.shard_map(body, mesh=mesh, in_specs=in_specs, out_specs=out_specs, check_vma=False)
```
